128 devices in a mesh: sub: 32 (over y, x, core), gy: 4 (over z).
Axes of the slice: x: 4, y: 4, z: 4, core: 2. Of those that a mesh axis runs over, the one named last changes fastest.
Arguments:
- a_vals: bfloat16 [64, 64, 64, 320], P('sub', 'gy'), may hold values from -0.75 to 0.75
- p_vals: bfloat16 [64, 64, 64, 128], P('sub', 'gy'), may hold values from -0.75 to 0.75
- spill_axis: int32 [64, 64], P('sub', 'gy'), may hold values from 0 to 1
Outputs:
- coarse: bfloat16 [32, 32, 64, 1600], P('sub', 'gy')
The draws below stay inside these ranges and needn't reach their ends.
Inputs may be any that keep to these rules, and one draw needn't show every extreme that they name: `spill_axis`: 0 puts the second aggregate across the nearer aggregate face along the slab, 1 across it.
All inputs are finite; a program needn't handle non-finite values.
Results may differ from the reference program's by a relative error of at most 0.007.
Values may be sent and summed in bfloat16 or wider, within the bound.
A program may use at most 384 MiB of HBM per device.

```python
import jax
import jax.numpy as jnp
from jax import lax

B = 64
CS = 2
SLOTS = 25
NS = 64
NG = 64
MS = 32
MG = 32
N_SUB = 32


def set_ends(entries, own_key, smallest, largest):
    longest = entries.shape.index(max(entries.shape))
    spots = []
    for shift in (0, 1):
        where = [jax.random.randint(jax.random.fold_in(own_key, axis), (), 0, length) for axis, length in enumerate(entries.shape)]
        where[longest] = (where[longest] + shift) % entries.shape[longest]
        spots.append(tuple(where))
    return entries.at[spots[0]].set(smallest).at[spots[1]].set(largest)


def block_scale(own_key, dims, split, smallest, top_value):
    level = 1.0
    for dim, shards_of in split:
        steps = jax.random.uniform(jax.random.fold_in(jax.random.fold_in(own_key, 6), dim), (shards_of,), jnp.float32, smallest / len(split), top_value / len(split))
        level = level * jnp.repeat(jnp.exp(steps), dims[dim] // shards_of).reshape((-1,) + (1,) * (len(dims) - 1 - dim))
    return level


def bell_draw(rng, shape, scale, most, split=(), kind=jnp.bfloat16):
    values = jax.random.normal(rng, shape, jnp.float32) * scale
    if len(split) > 0:
        values = block_scale(rng, shape, split, -0.22, 0.18) * values
    return jnp.clip(values, min=-most, max=most).astype(kind)


def setup_inputs(seed: int = 0) -> dict:
    key_list = jax.random.split(jax.random.key(seed), 4)
    return {
        "a_vals": bell_draw(key_list[0], (NS, NG, B, 5 * B), B ** -0.5, 0.75, ((0, 32), (1, 4))),
        "p_vals": bell_draw(key_list[1], (NS, NG, B, 2 * B), B ** -0.5, 0.75, ((0, 32), (1, 4))),
        "spill_axis": set_ends(jax.random.randint(key_list[2], (NS, NG), 0, 2), jax.random.fold_in(key_list[2], 1), 0, 1).astype(jnp.int32),
    }


OFFSETS = ((0, 0), (-1, 0), (1, 0), (0, -1), (0, 1))


def coarse_of(xs, ys, spill, which):
    step_s = jnp.where(spill == 0, 2 * (xs % 2) - 1, 0) * which
    step_g = jnp.where(spill == 1, 2 * (ys % 2) - 1, 0) * which
    return xs // 2 + step_s, ys // 2 + step_g


def assemble(acc, a_reg, p_ext, sp_ext, anchor_x, anchor_y, corner_x, corner_y, rows_c, cols_c, total_x, total_y):
    rows_f = a_reg.shape[0]
    cols_f = a_reg.shape[1]
    width = p_ext.shape[2]
    xs = anchor_x + jnp.arange(rows_f, dtype=jnp.int32)[:, None] + jnp.zeros((1, cols_f), jnp.int32)
    ys = anchor_y + jnp.zeros((rows_f, 1), jnp.int32) + jnp.arange(cols_f, dtype=jnp.int32)[None, :]
    own_p = p_ext[1:rows_f + 1, 1:cols_f + 1]
    own_sp = sp_ext[1:rows_f + 1, 1:cols_f + 1]
    left = own_p.astype(jnp.float32).reshape(rows_f, cols_f, width, 2, width)
    dump = acc.shape[0] - 1
    for k in range(5):
        shift_s, shift_g = OFFSETS[k]
        near_p = p_ext[1 + shift_s:1 + shift_s + rows_f, 1 + shift_g:1 + shift_g + cols_f]
        near_sp = sp_ext[1 + shift_s:1 + shift_s + rows_f, 1 + shift_g:1 + shift_g + cols_f]
        block_a = a_reg[:, :, :, k * width:(k + 1) * width]
        product = jnp.einsum('xyab,xybc->xyac', block_a.astype(jnp.float32), near_p.astype(jnp.float32)).astype(jnp.bfloat16)
        right = product.astype(jnp.float32).reshape(rows_f, cols_f, width, 2, width)
        terms = jnp.einsum('xybpa,xybqc->xypqac', left, right)
        rows_ids = []
        for which_p in range(2):
            agg_x, agg_y = coarse_of(xs, ys, own_sp, which_p)
            pair_ids = []
            for which_q in range(2):
                col_x, col_y = coarse_of(xs + shift_s, ys + shift_g, near_sp, which_q)
                valid = (agg_x >= 0) & (agg_x < total_x) & (agg_y >= 0) & (agg_y < total_y)
                valid = valid & (col_x >= 0) & (col_x < total_x) & (col_y >= 0) & (col_y < total_y)
                valid = valid & (agg_x - corner_x >= 0) & (agg_x - corner_x < rows_c)
                valid = valid & (agg_y - corner_y >= 0) & (agg_y - corner_y < cols_c)
                slot = (col_x - agg_x + 2) * 5 + (col_y - agg_y + 2)
                target = ((agg_x - corner_x) * cols_c + (agg_y - corner_y)) * SLOTS + slot
                pair_ids.append(jnp.where(valid, target, dump).astype(jnp.int32))
            rows_ids.append(jnp.stack(pair_ids, -1))
        targets = jnp.stack(rows_ids, -2).reshape(-1)
        acc = acc.at[targets].add(terms.reshape(-1, width * width))
    return acc


def reference(a_vals, p_vals, spill_axis):
    p_pad = jnp.pad(p_vals, ((1, 1), (1, 1), (0, 0), (0, 0)))
    sp_pad = jnp.pad(spill_axis, ((1, 1), (1, 1)))
    acc = jnp.zeros(((MS + 2) * (MG + 2) * SLOTS + 1, B * B), jnp.float32)

    def strip(index, acc):
        start = (index * CS).astype(jnp.int32)
        a_strip = lax.dynamic_slice_in_dim(a_vals, start, CS, 0)
        p_strip = lax.dynamic_slice_in_dim(p_pad, start, CS + 2, 0)
        sp_strip = lax.dynamic_slice_in_dim(sp_pad, start, CS + 2, 0)
        return assemble(acc, a_strip, p_strip, sp_strip, start, jnp.int32(0), jnp.int32(-1), jnp.int32(-1), MS + 2, MG + 2, MS, MG)

    acc = lax.fori_loop(0, N_SUB, strip, acc)
    whole = acc[:-1].reshape(MS + 2, MG + 2, SLOTS, B, B)[1:-1, 1:-1]
    return whole.transpose(0, 1, 3, 2, 4).reshape(MS, MG, B, SLOTS * B).astype(jnp.bfloat16)
```

```python
import functools

import jax
import jax.numpy as jnp
from jax import lax
from jax.experimental import pallas as pl
from jax.experimental.pallas import tpu as pltpu
from jax.sharding import PartitionSpec as P

MESH = pl.DeviceIdType.MESH
F32 = jnp.float32
BF16 = jnp.bfloat16
B = 64
SLOTS = 25


def lanes_low(rows, dtype):
    lane = lax.broadcasted_iota(jnp.int32, (rows, 128), 1)
    return jnp.where(lane < B, 1.0, 0.0).astype(dtype)


def swap_halves(tile):
    return jnp.concatenate([tile[:, B:], tile[:, :B]], axis=1)


def tall(mask):
    return jnp.concatenate([mask] * 4, axis=0)


def transposed_dot(left, right):
    return lax.dot_general(left, right, (((0,), (0,)), ((), ())), preferred_element_type=F32)


def spread(row, cols):
    wide = jnp.broadcast_to(row, (cols, cols))
    at = lax.broadcasted_iota(jnp.int32, (cols, cols), 0)
    lane = lax.broadcasted_iota(jnp.int32, (cols, cols), 1)
    column = jnp.sum(jnp.where(at == lane, wide, 0.0), axis=1, keepdims=True)
    column = jnp.broadcast_to(column, (cols, 128))
    return jnp.broadcast_to(column[:, None, :], (cols, 16, 128))


def kernel(
    n_sub, n_gy, cols,
    a_hbm, p_hbm, sp_hbm, out,
    a_v, pe, sp_own, sp_h, m0t, m1t, rhs, la, lb, gs, msg, rmsg, acc, gl, gr,
    local_sem, sp_send, sp_recv, ps_send, ps_recv, pg_send, pg_recv,
    ms_send, ms_recv, mg_send, mg_recv,
):
    s = lax.axis_index("sub")
    z = lax.axis_index("gy")
    aggs = cols // 2
    chunks = aggs // 2
    before = lax.rem(s + n_sub - 1, n_sub)
    after = lax.rem(s + 1, n_sub)
    lower = lax.rem(z + n_gy - 1, n_gy)
    upper = lax.rem(z + 1, n_gy)
    around = ((before, z), (after, z), (s, lower), (s, upper))
    slow = lax.rem(s, 2)

    barrier = pltpu.get_barrier_semaphore()
    for device in around:
        pl.semaphore_signal(barrier, inc=1, device_id=device, device_id_type=MESH)
    get_sp = pltpu.make_async_copy(sp_hbm, sp_own, local_sem.at[0])
    get_p = pltpu.make_async_copy(p_hbm, pe.at[1:3, 1 : cols + 1], local_sem.at[1])
    get_a = pltpu.make_async_copy(a_hbm, a_v, local_sem.at[2])
    get_sp.start()
    get_p.start()
    get_a.start()
    pl.semaphore_wait(barrier, 4)

    def remote(src, dst, send, recv, device):
        return pltpu.make_async_remote_copy(
            src_ref=src, dst_ref=dst, send_sem=send, recv_sem=recv, device_id=device, device_id_type=MESH
        )

    sp_copies = [
        remote(sp_hbm, sp_h.at[d ^ 1], sp_send.at[d], sp_recv.at[d ^ 1], around[d]) for d in range(4)
    ]
    pg_copies = [
        remote(p_hbm.at[:, 0], pe.at[1:3, cols + 1], pg_send.at[0], pg_recv.at[1], around[2]),
        remote(p_hbm.at[:, cols - 1], pe.at[1:3, 0], pg_send.at[1], pg_recv.at[0], around[3]),
    ]

    def ps_copy(r, c):
        device = (lax.rem(s + n_sub - 1 + 2 * r, n_sub), z)
        return remote(
            p_hbm.at[r, pl.ds(4 * c, 4)], pe.at[3 * (1 - r), pl.ds(1 + 4 * c, 4)],
            ps_send.at[r, c], ps_recv.at[1 - r, c], device,
        )

    def ps_landing(r, c):
        device = (lax.rem(s + n_sub - 1 + 2 * r, n_sub), z)
        return remote(
            p_hbm.at[r, pl.ds(4 * c, 4)], pe.at[3 * r, pl.ds(1 + 4 * c, 4)],
            ps_send.at[r, c], ps_recv.at[r, c], device,
        )

    def ms_copy(r, c):
        device = (lax.rem(s + n_sub - 1 + 2 * r, n_sub), z)
        return remote(
            msg.at[r, c], rmsg.at[1 - r, c], ms_send.at[r, c], ms_recv.at[1 - r, c], device
        )

    def ms_landing(r, c):
        device = (lax.rem(s + n_sub - 1 + 2 * r, n_sub), z)
        return remote(msg.at[r, c], rmsg.at[r, c], ms_send.at[r, c], ms_recv.at[r, c], device)

    for copy in sp_copies:
        copy.start()
    for copy in pg_copies:
        copy.start()
    for c in range(chunks):
        ps_copy(slow, c).start()
        ps_copy(1 - slow, c).start()

    lo = lanes_low(16, BF16)
    hi = (1.0 - lanes_low(16, F32)).astype(BF16)
    lo32 = lanes_low(B, F32)
    zero = jnp.zeros((B, 128), BF16)

    def flag(condition):
        return jnp.where(condition, 1.0, 0.0).astype(F32)

    has_before, has_after = flag(s > 0), flag(s < n_sub - 1)
    has_lower, has_upper = flag(z > 0), flag(z < n_gy - 1)

    for g in range(aggs):
        for t in (0, 2, 10):
            out[0, g, :, 128 * t : 128 * t + 128] = zero
        out[0, g, :, 1536:] = jnp.zeros((B, B), BF16)
        gs[g, 4, 0] = jnp.zeros((128, 128), BF16)
        gs[g, 3, 1] = jnp.zeros((128, 128), BF16)

    column = lax.broadcasted_iota(jnp.int32, (1, cols), 1)
    side_ok = jnp.where(column == 0, has_lower, jnp.where(column == cols - 1, has_upper, 1.0))

    def masks_of_row(row, e, here, reach):
        m0t[e, 1 : cols + 1] = spread((1.0 - row) * (reach * here), cols).astype(BF16)
        m1t[e, 1 : cols + 1] = spread(row * side_ok * here, cols).astype(BF16)

    get_sp.wait()
    own = sp_own[...].astype(F32)
    masks_of_row(own[0:1], 1, F32(1.0), has_before)
    masks_of_row(own[1:2], 2, F32(1.0), has_after)
    get_p.wait()

    def prepare(t, carry):
        r = lax.div(t, aggs)
        g = lax.rem(t, aggs)
        k_in = 2 - r
        for odd in range(2):
            y = 2 * g + odd
            tile = pe[1 + r, 1 + y]
            turned = swap_halves(tile)
            m0 = m0t[1 + r, 1 + y]
            m1 = m1t[1 + r, 1 + y]
            first = turned * tall(m0 * lo)
            only = turned * tall(m1 * lo)
            plain = turned * tall(hi)
            second = only + plain if odd == 0 else plain
            third = zero if odd == 0 else only
            for where_y, k, parts in (
                (y, 0, (first, second, third, zero)),
                (y + 1 - 2 * odd, 4 - (1 - odd), (first, second, third, zero)),
            ):
                for n, part in enumerate(parts):
                    rhs[r, 1 + where_y, k, :, 128 * n : 128 * n + 128] = part
            for n, part in enumerate((zero, second, third, first)):
                rhs[1 - r, 1 + y, 1 + r, :, 128 * n : 128 * n + 128] = part
            if odd == 0:
                outer = (tile * tall(m0 * hi), tile * tall(m1 * hi), tile * tall(lo), zero)
                out_y, out_k = y - 1, 4
            else:
                outer = (zero, tile * tall(lo + m1 * hi), tile * tall(m0 * hi), zero)
                out_y, out_k = y + 1, 3
            for n, part in enumerate(outer):
                rhs[r, 1 + out_y, out_k, :, 128 * n : 128 * n + 128] = part
            la[r, g, B * odd : B * odd + B] = first[:, :B]
            if odd == 0:
                lb[g, r, 0:B, 0:128] = tile * tall(lo + m1 * hi)
                lb[g, r, 0:B, 128:192] = zero[:, :B]
            else:
                lb[g, r, B : 2 * B, 0:128] = tile * tall(lo)
                lb[g, r, B : 2 * B, 128:192] = only[:, :B]
        return carry

    lax.fori_loop(0, 2 * aggs, prepare, 0)

    for copy in sp_copies:
        copy.wait_recv()
    masks_of_row(sp_h[0, 1:2].astype(F32), 0, has_before, F32(1.0))
    masks_of_row(sp_h[1, 0:1].astype(F32), 3, has_after, F32(1.0))
    for copy in pg_copies:
        copy.wait_recv()
    for r, reach in ((0, has_before), (1, has_after)):
        low = jnp.broadcast_to(sp_h[2, r : r + 1, cols - 1 : cols].astype(F32), (16, 128))
        m0 = ((1.0 - low) * (reach * has_lower)).astype(BF16)
        m1 = (low * has_lower).astype(BF16)
        here = jnp.broadcast_to(has_lower, (16, 128)).astype(BF16)
        tile = pe[1 + r, 0]
        for n, part in enumerate((zero, tile * tall(lo * here + m1 * hi), tile * tall(m0 * hi), zero)):
            rhs[r, 1, 3, :, 128 * n : 128 * n + 128] = part
        high = jnp.broadcast_to(sp_h[3, r : r + 1, 0:1].astype(F32), (16, 128))
        m0 = ((1.0 - high) * (reach * has_upper)).astype(BF16)
        m1 = (high * has_upper).astype(BF16)
        here = jnp.broadcast_to(has_upper, (16, 128)).astype(BF16)
        tile = pe[1 + r, cols + 1]
        for n, part in enumerate((tile * tall(m0 * hi), tile * tall(m1 * hi), tile * tall(lo * here), zero)):
            rhs[r, cols, 4, :, 128 * n : 128 * n + 128] = part
    get_a.wait()

    def sweep(t, carry):
        c = lax.div(t, 2)
        r = lax.rem(slow + lax.rem(t, 2), 2)
        ps_landing(r, c).wait_recv()
        present = jnp.where(r == 0, has_before, has_after)
        here = lo * jnp.broadcast_to(present, (16, 128)).astype(BF16)
        last = []
        for i in range(2):
            g = 2 * c + i
            for odd in range(2):
                y = 2 * g + odd
                tile = pe[3 * r, 1 + y]
                m0 = m0t[3 * r, 1 + y]
                m1 = m1t[3 * r, 1 + y]
                middle = tile * tall(m0 * hi)
                if odd == 0:
                    parts = (tile * tall(here), middle, tile * tall(m1 * hi), zero)
                else:
                    parts = (tile * tall(here + m1 * hi), middle, zero, zero)
                for n, part in enumerate(parts):
                    rhs[r, 1 + y, 1 + r, :, 128 * n : 128 * n + 128] = part
                right = rhs[r, 1 + y].reshape(5 * B, 512)
                left = a_v[r, y]
                made = jnp.dot(left[:, :256], right[:256], preferred_element_type=F32)
                made += jnp.dot(left[:, 256:], right[256:], preferred_element_type=F32)
                made = made.astype(BF16)
                for n, place in enumerate((r, 2, 3 + r, 1 - r)):
                    gs[g, place, r, B * odd : B * odd + B] = made[:, 128 * n : 128 * n + 128]
            right = jnp.concatenate([gs[g, place, r] for place in (r, 2, 3 + r, 1 - r)], axis=1)
            leave = transposed_dot(la[r, g], right)
            for n in range(3):
                msg[r, c, 3 * i + n] = leave[:, 128 * n : 128 * n + 128].astype(BF16)
            last.append(leave[:, 384:512])
        msg[r, c, 6] = jnp.concatenate([last[0][:, :B], last[1][:, :B]], axis=1).astype(BF16)
        ms_copy(r, c).start()
        return carry

    lax.fori_loop(0, 2 * chunks, sweep, 0)

    mg_copies = [
        remote(gr.at[0], gr.at[aggs], mg_send.at[0], mg_recv.at[1], around[2]),
        remote(gl.at[aggs], gl.at[0], mg_send.at[1], mg_recv.at[0], around[3]),
    ]

    def gather(t, carry):
        g = lax.rem(t + aggs - 1, aggs)
        right = jnp.concatenate([gs[g, n].reshape(256, 128) for n in range(5)], axis=1)
        made = transposed_dot(lb[g].reshape(256, 192), right)

        def piece(rows, n):
            return made[B * rows : B * rows + B, 128 * n : 128 * n + 128]

        low = lo32 > 0.5
        um, up, ce, d0, d1 = (swap_halves(piece(0, n)) for n in range(5))
        acc[g, 0] = jnp.where(low, d0, um)
        acc[g, 1] = jnp.where(low, um, 0.0)
        acc[g, 2] = jnp.where(low, 0.0, ce)
        acc[g, 3] = jnp.where(low, ce, d0 + d1)
        acc[g, 4] = jnp.where(low, d1, up)
        acc[g, 5] = jnp.where(low, up, 0.0)
        um, up, ce, d0, d1 = (piece(1, n) for n in range(5))
        gr[g, 0] = jnp.where(low, um, d0).astype(BF16)
        gr[g, 1] = jnp.where(low, up, d1).astype(BF16)
        gr[g, 2] = ce.astype(BF16)
        gr[g, 3] = jnp.where(low, d0 + d1, 0.0).astype(BF16)
        um, up, ce, d0, d1 = (piece(2, n) for n in range(5))
        gl[g + 1, 0] = um.astype(BF16)
        gl[g + 1, 1] = up.astype(BF16)
        gl[g + 1, 2] = ce.astype(BF16)
        gl[g + 1, 3] = (d0 + d1).astype(BF16)

        @pl.when(t == 1)
        def _():
            for copy in mg_copies:
                copy.start()

        return carry

    lax.fori_loop(0, aggs, gather, 0)
    for copy in mg_copies:
        copy.wait_recv()

    def finish(c, carry):
        low = lo32 > 0.5
        ms_landing(1 - slow, c).wait_recv()
        ms_landing(slow, c).wait_recv()
        for i in range(2):
            g = 2 * c + i
            b0, b1, b2 = (rmsg[0, c, 3 * i + n].astype(F32) for n in range(3))
            f0, f1, f2 = (rmsg[1, c, 3 * i + n].astype(F32) for n in range(3))
            b3, f3 = rmsg[0, c, 6].astype(F32), rmsg[1, c, 6].astype(F32)
            if i == 1:
                b3, f3 = swap_halves(b3), swap_halves(f3)
            l0, l1, l2, l3 = (gl[g, n].astype(F32) for n in range(4))
            r0, r1, r2, r3 = (gr[g + 1, n].astype(F32) for n in range(4))
            tiles = (
                (1, jnp.where(low, b3, 0.0)),
                (3, acc[g, 0] + b1 + l0 + jnp.where(low, 0.0, r0)),
                (4, acc[g, 1] + jnp.where(low, b2 + r0, 0.0)),
                (5, acc[g, 2] + l2 + jnp.where(low, 0.0, b2 + f2)),
                (6, acc[g, 3] + b0 + f0 + l3 + r2),
                (7, r3),
                (8, acc[g, 4] + f1 + l1 + jnp.where(low, 0.0, r1)),
                (9, acc[g, 5] + jnp.where(low, f2 + r1, 0.0)),
                (11, jnp.where(low, f3, 0.0)),
            )
            for t, value in tiles:
                out[0, g, :, 128 * t : 128 * t + 128] = value.astype(BF16)
        return carry

    lax.fori_loop(0, chunks, finish, 0)

    for copy in sp_copies + pg_copies + mg_copies:
        copy.wait_send()
    for r in range(2):
        for c in range(chunks):
            ps_copy(r, c).wait_send()
            ms_copy(r, c).wait_send()


def local(a_vals, p_vals, spill_axis):
    n_sub = lax.axis_size("sub")
    n_gy = lax.axis_size("gy")
    cols = a_vals.shape[1]
    aggs = cols // 2
    chunks = aggs // 2
    dma = pltpu.SemaphoreType.DMA
    return pl.pallas_call(
        functools.partial(kernel, n_sub, n_gy, cols),
        out_shape=jax.ShapeDtypeStruct((1, aggs, B, SLOTS * B), BF16),
        in_specs=[pl.BlockSpec(memory_space=pl.ANY)] * 3,
        out_specs=pl.BlockSpec(memory_space=pltpu.VMEM),
        scratch_shapes=[
            pltpu.VMEM((2, cols, B, 5 * B), BF16),
            pltpu.VMEM((4, cols + 2, B, 128), BF16),
            pltpu.VMEM((2, cols), jnp.int32),
            pltpu.VMEM((4, 2, cols), jnp.int32),
            pltpu.VMEM((4, cols + 2, 16, 128), BF16),
            pltpu.VMEM((4, cols + 2, 16, 128), BF16),
            pltpu.VMEM((2, cols + 2, 5, B, 512), BF16),
            pltpu.VMEM((2, aggs, 128, B), BF16),
            pltpu.VMEM((aggs, 2, 128, 192), BF16),
            pltpu.VMEM((aggs, 5, 2, 128, 128), BF16),
            pltpu.VMEM((2, chunks, 7, B, 128), BF16),
            pltpu.VMEM((2, chunks, 7, B, 128), BF16),
            pltpu.VMEM((aggs, 6, B, 128), F32),
            pltpu.VMEM((aggs + 1, 4, B, 128), BF16),
            pltpu.VMEM((aggs + 1, 4, B, 128), BF16),
            dma((3,)),
            dma((4,)),
            dma((4,)),
            dma((2, chunks)),
            dma((2, chunks)),
            dma((2,)),
            dma((2,)),
            dma((2, chunks)),
            dma((2, chunks)),
            dma((2,)),
            dma((2,)),
        ],
        compiler_params=pltpu.CompilerParams(
            collective_id=0, has_side_effects=True, vmem_limit_bytes=48 * 1024 * 1024
        ),
        cost_estimate=pl.CostEstimate(flops=1_300_000_000, bytes_accessed=4_000_000, transcendentals=0),
    )(a_vals, p_vals, spill_axis)


def solution(mesh):
    return jax.shard_map(
        local,
        mesh=mesh,
        in_specs=(P("sub", "gy", None, None), P("sub", "gy", None, None), P("sub", "gy")),
        out_specs=P("sub", "gy", None, None),
        check_vma=False,
    )
```

```python
import functools

import jax
import jax.numpy as jnp
from jax import lax
from jax.experimental import pallas as pl
from jax.experimental.pallas import tpu as pltpu
from jax.sharding import PartitionSpec as P

MESH = pl.DeviceIdType.MESH
F32 = jnp.float32
BF16 = jnp.bfloat16
B = 64
SLOTS = 25


def lanes_low(rows, dtype):
    lane = lax.broadcasted_iota(jnp.int32, (rows, 128), 1)
    return jnp.where(lane < B, 1.0, 0.0).astype(dtype)


def swap_halves(tile):
    return jnp.concatenate([tile[:, B:], tile[:, :B]], axis=1)


def tall(mask):
    return jnp.concatenate([mask] * 4, axis=0)


def spread(row, cols):
    wide = jnp.broadcast_to(row, (cols, cols))
    at = lax.broadcasted_iota(jnp.int32, (cols, cols), 0)
    lane = lax.broadcasted_iota(jnp.int32, (cols, cols), 1)
    column = jnp.sum(jnp.where(at == lane, wide, 0.0), axis=1, keepdims=True)
    column = jnp.broadcast_to(column, (cols, 128))
    return jnp.broadcast_to(column[:, None, :], (cols, 16, 128)).astype(BF16)


def beside(tiles):
    return jnp.concatenate(tiles, axis=1)


def below(tiles):
    return jnp.concatenate(tiles, axis=0)


def kernel(
    n_sub, n_gy, cols,
    a_hbm, p_hbm, sp_hbm, out,
    a_v, pe, sp_own, sp_h, m0t, m1t, turn, flip, gs, msg, rmsg, acc, gl, gr,
    local_sem, sp_send, sp_recv, ps_send, ps_recv, pg_send, pg_recv,
    ms_send, ms_recv, mg_send, mg_recv,
):
    s = lax.axis_index("sub")
    z = lax.axis_index("gy")
    aggs = cols // 2
    chunks = aggs // 2
    around = (
        (lax.rem(s + n_sub - 1, n_sub), z),
        (lax.rem(s + 1, n_sub), z),
        (s, lax.rem(z + n_gy - 1, n_gy)),
        (s, lax.rem(z + 1, n_gy)),
    )
    there = (s > 0, s < n_sub - 1, z > 0, z < n_gy - 1)
    slow = lax.rem(s, 2)

    barrier = pltpu.get_barrier_semaphore()
    for d in range(4):

        @pl.when(there[d])
        def _():
            pl.semaphore_signal(barrier, inc=1, device_id=around[d], device_id_type=MESH)

    get_sp = pltpu.make_async_copy(sp_hbm, sp_own, local_sem.at[0])
    get_p = pltpu.make_async_copy(p_hbm, pe.at[1:3, 1 : cols + 1], local_sem.at[1])
    get_a = pltpu.make_async_copy(a_hbm, a_v, local_sem.at[2])
    get_sp.start()
    get_p.start()
    get_a.start()
    ones = [jnp.where(t, 1, 0).astype(jnp.int32) for t in there]
    pl.semaphore_wait(barrier, ones[0] + ones[1] + ones[2] + ones[3])

    def remote(src, dst, send, recv, device):
        return pltpu.make_async_remote_copy(
            src_ref=src, dst_ref=dst, send_sem=send, recv_sem=recv, device_id=device, device_id_type=MESH
        )

    def sp_copy(d, landing=False):
        e = d if landing else d ^ 1
        return remote(sp_hbm, sp_h.at[e], sp_send.at[d], sp_recv.at[e], around[d])

    def pg_copy(d, landing=False):
        e = d if landing else d ^ 1
        return remote(
            p_hbm.at[:, (cols - 1) * (d - 2)], pe.at[1:3, (cols + 1) * (e - 2)],
            pg_send.at[d - 2], pg_recv.at[e - 2], around[d],
        )

    def ps_copy(d, c, landing=False):
        e = d if landing else d ^ 1
        return remote(
            p_hbm.at[d, pl.ds(4 * c, 4)], pe.at[3 * e, pl.ds(1 + 4 * c, 4)],
            ps_send.at[d, c], ps_recv.at[e, c], around[d],
        )

    def ms_copy(d, c, landing=False):
        e = d if landing else d ^ 1
        return remote(msg.at[d, c], rmsg.at[e, c], ms_send.at[d, c], ms_recv.at[e, c], around[d])

    mg_copies = {
        2: remote(gr.at[0], gr.at[aggs], mg_send.at[0], mg_recv.at[1], around[2]),
        3: remote(gl.at[aggs], gl.at[0], mg_send.at[1], mg_recv.at[0], around[3]),
    }
    mg_landing = {
        2: remote(gl.at[aggs], gl.at[0], mg_send.at[0], mg_recv.at[0], around[2]),
        3: remote(gr.at[0], gr.at[aggs], mg_send.at[1], mg_recv.at[1], around[3]),
    }

    for d in range(4):

        @pl.when(there[d])
        def _():
            sp_copy(d).start()

    for d in (2, 3):

        @pl.when(there[d])
        def _():
            pg_copy(d).start()

    for d in (0, 1):

        @pl.when(there[d])
        def _():
            for c in range(chunks):
                ps_copy(d, c).start()

    tile0 = jnp.zeros((B, 128), BF16)
    for d in range(4):

        @pl.when(jnp.logical_not(there[d]))
        def _():
            sp_h[d] = jnp.zeros((2, cols), jnp.int32)
            if d < 2:
                for y in range(cols):
                    pe[3 * d, 1 + y] = tile0
                for c in range(chunks):
                    for n in range(7):
                        rmsg[d, c, n] = tile0
            else:
                for r in range(2):
                    pe[1 + r, (cols + 1) * (d - 2)] = tile0
                for n in range(4):
                    if d == 2:
                        gl[0, n] = tile0
                    else:
                        gr[aggs, n] = tile0

    lo = lanes_low(16, BF16)
    hi = (1.0 - lanes_low(16, F32)).astype(BF16)
    lo32 = lanes_low(B, F32)

    def flag(condition, rows=16):
        return jnp.broadcast_to(jnp.where(condition, 1.0, 0.0).astype(F32), (rows, 128)).astype(BF16)

    reach = (flag(there[0]), flag(there[1]))
    side = (flag(there[2]), flag(there[3]))

    for g in range(aggs):
        for t in (0, 2, 10):
            out[0, g, :, 128 * t : 128 * t + 128] = tile0
        out[0, g, :, 1536:] = jnp.zeros((B, B), BF16)
        gs[g, 4, 0] = jnp.zeros((128, 128), BF16)
        gs[g, 3, 1] = jnp.zeros((128, 128), BF16)

    def masks_of_row(row, e):
        spill = spread(row, cols)
        straight = 1.0 - spill
        m0t[e, 1 : cols + 1] = straight if e in (0, 3) else straight * reach[e - 1][None]
        m1t[e, 2:cols] = spill[1 : cols - 1]
        m1t[e, 1] = spill[0] * side[0]
        m1t[e, cols] = spill[cols - 1] * side[1]

    get_sp.wait()
    own = sp_own[...].astype(F32)
    masks_of_row(own[0:1], 1)
    masks_of_row(own[1:2], 2)
    get_p.wait()

    def prepare(t, carry):
        for r in range(2):
            pair = []
            for odd in range(2):
                y = 2 * t + odd
                tile = pe[1 + r, 1 + y]
                turn[r, y] = swap_halves(tile)
                pair.append(tile)
            flip[r, t] = below(pair).T
        return carry

    lax.fori_loop(0, aggs, prepare, 0)

    for d in range(4):

        @pl.when(there[d])
        def _():
            sp_copy(d, True).wait_recv()

    masks_of_row(sp_h[0, 1:2].astype(F32), 0)
    masks_of_row(sp_h[1, 0:1].astype(F32), 3)
    for d, at, column in ((2, 0, cols - 1), (3, cols + 1, 0)):
        for r in range(2):
            spill = jnp.broadcast_to(sp_h[d, r : r + 1, column : column + 1].astype(F32), (16, 128)).astype(BF16)
            m0t[1 + r, at] = (1.0 - spill) * reach[r]
            m1t[1 + r, at] = spill

    for d in (2, 3):

        @pl.when(there[d])
        def _():
            pg_copy(d, True).wait_recv()

    get_a.wait()

    def inner(r, y, odd):
        tile = turn[r, y]
        m0, m1 = m0t[1 + r, 1 + y], m1t[1 + r, 1 + y]
        first = tile * tall(m0 * lo)
        if odd == 0:
            return first, tile * tall(m1 * lo + hi), tile0
        return first, tile * tall(hi), tile * tall(m1 * lo)

    def sweep(r, c):
        @pl.when(there[r])
        def _():
            ps_copy(r, c, True).wait_recv()

        last = []
        for i in range(2):
            g = 2 * c + i
            own = [inner(r, 2 * g + odd, odd) for odd in range(2)]
            made = []
            for odd in range(2):
                y = 2 * g + odd
                first, second, third = inner(1 - r, y, odd)
                x_in = beside([tile0, second, third, first])
                tile = pe[3 * r, 1 + y]
                m0, m1 = m0t[3 * r, 1 + y], m1t[3 * r, 1 + y]
                middle = tile * tall(m0 * hi)
                if odd == 0:
                    x_out = beside([tile * tall(lo), middle, tile * tall(m1 * hi), tile0])
                else:
                    x_out = beside([tile * tall(lo + m1 * hi), middle, tile0, tile0])
                at = y - 1 + 2 * odd
                tile = pe[1 + r, 1 + at]
                m0, m1 = m0t[1 + r, 1 + at], m1t[1 + r, 1 + at]
                if odd == 0:
                    y_out = beside([tile0, tile * tall(lo + m1 * hi), tile * tall(m0 * hi), tile0])
                else:
                    y_out = beside([tile * tall(m0 * hi), tile * tall(m1 * hi), tile * tall(lo), tile0])
                y_in = beside([*own[1 - odd], tile0])
                blocks = [beside([*own[odd], tile0])]
                blocks += [x_out, x_in] if r == 0 else [x_in, x_out]
                blocks += [y_out, y_in] if odd == 0 else [y_in, y_out]
                left = a_v[r, y]
                value = jnp.dot(left[:, :256], below(blocks[:4]), preferred_element_type=F32)
                value += jnp.dot(left[:, 256:], blocks[4], preferred_element_type=F32)
                made.append(value.astype(BF16))
            right = below(made)
            m0 = [m0t[1 + r, 1 + 2 * g + odd] for odd in range(2)]
            leave = jnp.dot(
                flip[r, g, B:] * tall(m0[0] * lo + m0[1] * hi), right, preferred_element_type=F32
            )
            for n, place in enumerate((r, 2, 3 + r, 1 - r)):
                gs[g, place, r] = right[:, 128 * n : 128 * n + 128]
            for n in range(3):
                msg[r, c, 3 * i + n] = leave[:, 128 * n : 128 * n + 128].astype(BF16)
            last.append(leave[:, 384:512])
        msg[r, c, 6] = beside([last[0][:, :B], last[1][:, :B]]).astype(BF16)

        @pl.when(there[r])
        def _():
            ms_copy(r, c).start()

    for behind in range(2):

        @pl.when(slow == behind)
        def _():
            def step(c, carry):
                sweep(1 - behind, c)
                sweep(behind, c)
                return carry

            lax.fori_loop(0, chunks, step, 0)

    low = lo32 > 0.5

    def gather(t, carry):
        g = lax.rem(t + aggs - 1, aggs)
        right = beside([gs[g, n].reshape(256, 128) for n in range(5)])
        m1 = [[m1t[1 + r, 1 + 2 * g + odd] for odd in range(2)] for r in range(2)]
        left = below([
            beside([flip[r, g, :B] for r in range(2)]),
            beside([flip[r, g, B:] * tall(m1[r][0] * lo) for r in range(2)]),
            beside([flip[r, g, B:] * tall(m1[r][1] * hi) for r in range(2)]),
        ])
        made = jnp.dot(left, right, preferred_element_type=F32)

        def piece(rows, n):
            return made[B * rows : B * rows + B, 128 * n : 128 * n + 128]

        um, up, ce, d0, d1 = (swap_halves(piece(0, n)) for n in range(5))
        acc[g, 0] = jnp.where(low, d0, um)
        acc[g, 1] = jnp.where(low, um, 0.0)
        acc[g, 2] = jnp.where(low, 0.0, ce)
        acc[g, 3] = jnp.where(low, ce, d0 + d1)
        acc[g, 4] = jnp.where(low, d1, up)
        acc[g, 5] = jnp.where(low, up, 0.0)
        um, up, ce, d0, d1 = (piece(1, n) for n in range(5))
        gr[g, 0] = jnp.where(low, um, d0).astype(BF16)
        gr[g, 1] = jnp.where(low, up, d1).astype(BF16)
        gr[g, 2] = ce.astype(BF16)
        gr[g, 3] = jnp.where(low, d0 + d1, 0.0).astype(BF16)
        um, up, ce, d0, d1 = (piece(2, n) for n in range(5))
        gl[g + 1, 0] = um.astype(BF16)
        gl[g + 1, 1] = up.astype(BF16)
        gl[g + 1, 2] = ce.astype(BF16)
        gl[g + 1, 3] = (d0 + d1).astype(BF16)

        @pl.when(t == 1)
        def _():
            for d in (2, 3):

                @pl.when(there[d])
                def _():
                    mg_copies[d].start()

        return carry

    lax.fori_loop(0, aggs, gather, 0)
    for d in (2, 3):

        @pl.when(there[d])
        def _():
            mg_landing[d].wait_recv()

    def finish(c, carry):
        for d in range(2):

            @pl.when(there[d])
            def _():
                ms_copy(d, c, True).wait_recv()

        for i in range(2):
            g = 2 * c + i
            b0, b1, b2 = (rmsg[0, c, 3 * i + n].astype(F32) for n in range(3))
            f0, f1, f2 = (rmsg[1, c, 3 * i + n].astype(F32) for n in range(3))
            b3, f3 = rmsg[0, c, 6].astype(F32), rmsg[1, c, 6].astype(F32)
            if i == 1:
                b3, f3 = swap_halves(b3), swap_halves(f3)
            l0, l1, l2, l3 = (gl[g, n].astype(F32) for n in range(4))
            r0, r1, r2, r3 = (gr[g + 1, n].astype(F32) for n in range(4))
            tiles = (
                (1, jnp.where(low, b3, 0.0)),
                (3, acc[g, 0] + b1 + l0 + jnp.where(low, 0.0, r0)),
                (4, acc[g, 1] + jnp.where(low, b2 + r0, 0.0)),
                (5, acc[g, 2] + l2 + jnp.where(low, 0.0, b2 + f2)),
                (6, acc[g, 3] + b0 + f0 + l3 + r2),
                (7, r3),
                (8, acc[g, 4] + f1 + l1 + jnp.where(low, 0.0, r1)),
                (9, acc[g, 5] + jnp.where(low, f2 + r1, 0.0)),
                (11, jnp.where(low, f3, 0.0)),
            )
            for t, value in tiles:
                out[0, g, :, 128 * t : 128 * t + 128] = value.astype(BF16)
        return carry

    lax.fori_loop(0, chunks, finish, 0)

    for d in range(4):

        @pl.when(there[d])
        def _():
            sp_copy(d).wait_send()
            if d < 2:
                for c in range(chunks):
                    ps_copy(d, c).wait_send()
                    ms_copy(d, c).wait_send()
            else:
                pg_copy(d).wait_send()
                mg_copies[d].wait_send()


def local(a_vals, p_vals, spill_axis):
    n_sub = lax.axis_size("sub")
    n_gy = lax.axis_size("gy")
    cols = a_vals.shape[1]
    aggs = cols // 2
    chunks = aggs // 2
    dma = pltpu.SemaphoreType.DMA
    return pl.pallas_call(
        functools.partial(kernel, n_sub, n_gy, cols),
        out_shape=jax.ShapeDtypeStruct((1, aggs, B, SLOTS * B), BF16),
        in_specs=[pl.BlockSpec(memory_space=pl.ANY)] * 3,
        out_specs=pl.BlockSpec(memory_space=pltpu.VMEM),
        scratch_shapes=[
            pltpu.VMEM((2, cols, B, 5 * B), BF16),
            pltpu.VMEM((4, cols + 2, B, 128), BF16),
            pltpu.VMEM((2, cols), jnp.int32),
            pltpu.VMEM((4, 2, cols), jnp.int32),
            pltpu.VMEM((4, cols + 2, 16, 128), BF16),
            pltpu.VMEM((4, cols + 2, 16, 128), BF16),
            pltpu.VMEM((2, cols, B, 128), BF16),
            pltpu.VMEM((2, aggs, 128, 128), BF16),
            pltpu.VMEM((aggs, 5, 2, 128, 128), BF16),
            pltpu.VMEM((2, chunks, 7, B, 128), BF16),
            pltpu.VMEM((2, chunks, 7, B, 128), BF16),
            pltpu.VMEM((aggs, 6, B, 128), F32),
            pltpu.VMEM((aggs + 1, 4, B, 128), BF16),
            pltpu.VMEM((aggs + 1, 4, B, 128), BF16),
            dma((3,)),
            dma((4,)),
            dma((4,)),
            dma((2, chunks)),
            dma((2, chunks)),
            dma((2,)),
            dma((2,)),
            dma((2, chunks)),
            dma((2, chunks)),
            dma((2,)),
            dma((2,)),
        ],
        compiler_params=pltpu.CompilerParams(
            collective_id=0, has_side_effects=True, vmem_limit_bytes=40 * 1024 * 1024
        ),
        cost_estimate=pl.CostEstimate(flops=1_300_000_000, bytes_accessed=4_000_000, transcendentals=0),
    )(*(pltpu.with_memory_space_constraint(x, pltpu.HBM) for x in (a_vals, p_vals, spill_axis)))


def solution(mesh):
    return jax.shard_map(
        local,
        mesh=mesh,
        in_specs=(P("sub", "gy", None, None), P("sub", "gy", None, None), P("sub", "gy")),
        out_specs=P("sub", "gy", None, None),
        check_vma=False,
    )
```

```python
import functools

import jax
import jax.numpy as jnp
from jax import lax
from jax.experimental import pallas as pl
from jax.experimental.pallas import tpu as pltpu
from jax.sharding import PartitionSpec as P

MESH = pl.DeviceIdType.MESH
F32 = jnp.float32
BF16 = jnp.bfloat16
B = 64
SLOTS = 25


def lanes_low(rows, dtype):
    lane = lax.broadcasted_iota(jnp.int32, (rows, 128), 1)
    return jnp.where(lane < B, 1.0, 0.0).astype(dtype)


def swap_halves(tile):
    return jnp.concatenate([tile[:, B:], tile[:, :B]], axis=1)


def tall(mask):
    return jnp.concatenate([mask] * 4, axis=0)


def spread(row, cols):
    wide = jnp.broadcast_to(row, (cols, cols))
    at = lax.broadcasted_iota(jnp.int32, (cols, cols), 0)
    lane = lax.broadcasted_iota(jnp.int32, (cols, cols), 1)
    column = jnp.sum(jnp.where(at == lane, wide, 0.0), axis=1, keepdims=True)
    column = jnp.broadcast_to(column, (cols, 128))
    return jnp.broadcast_to(column[:, None, :], (cols, 16, 128)).astype(BF16)


def beside(tiles):
    return jnp.concatenate(tiles, axis=1)


def below(tiles):
    return jnp.concatenate(tiles, axis=0)


def kernel(
    n_sub, n_gy, cols,
    a_hbm, p_hbm, sp_hbm, out,
    a_v, pe, sp_own, sp_h, m0t, m1t, turn, flip, part, gs, msg, rmsg, acc, gl, gr,
    local_sem, sp_send, sp_recv, ps_send, ps_recv, pg_send, pg_recv,
    ms_send, ms_recv, mg_send, mg_recv,
):
    s = lax.axis_index("sub")
    z = lax.axis_index("gy")
    aggs = cols // 2
    chunks = aggs // 2
    around = (
        (lax.rem(s + n_sub - 1, n_sub), z),
        (lax.rem(s + 1, n_sub), z),
        (s, lax.rem(z + n_gy - 1, n_gy)),
        (s, lax.rem(z + 1, n_gy)),
    )
    there = (s > 0, s < n_sub - 1, z > 0, z < n_gy - 1)
    slow = lax.rem(s, 2)
    order = [0, chunks - 1, *range(1, chunks - 1)]

    barrier = pltpu.get_barrier_semaphore()
    for d in range(4):

        @pl.when(there[d])
        def _():
            pl.semaphore_signal(barrier, inc=1, device_id=around[d], device_id_type=MESH)

    get_sp = pltpu.make_async_copy(sp_hbm, sp_own, local_sem.at[0])
    get_p = pltpu.make_async_copy(p_hbm, pe.at[1:3, 1 : cols + 1], local_sem.at[1])
    get_a = pltpu.make_async_copy(a_hbm, a_v, local_sem.at[2])
    get_sp.start()
    get_p.start()
    get_a.start()
    get_sp.wait()
    get_p.wait()
    ones = [jnp.where(t, 1, 0).astype(jnp.int32) for t in there]
    pl.semaphore_wait(barrier, ones[0] + ones[1] + ones[2] + ones[3])

    def remote(src, dst, send, recv, device):
        return pltpu.make_async_remote_copy(
            src_ref=src, dst_ref=dst, send_sem=send, recv_sem=recv, device_id=device, device_id_type=MESH
        )

    def sp_copy(d, landing=False):
        e = d if landing else d ^ 1
        return remote(sp_own, sp_h.at[e], sp_send.at[d], sp_recv.at[e], around[d])

    def pg_copy(d, landing=False):
        e = d if landing else d ^ 1
        return remote(
            pe.at[1:3, 1 + (cols - 1) * (d - 2)], pe.at[1:3, (cols + 1) * (e - 2)],
            pg_send.at[d - 2], pg_recv.at[e - 2], around[d],
        )

    def ps_copy(d, c, landing=False):
        e = d if landing else d ^ 1
        return remote(
            pe.at[1 + d, pl.ds(1 + 4 * c, 4)], pe.at[3 * e, pl.ds(1 + 4 * c, 4)],
            ps_send.at[d, c], ps_recv.at[e, c], around[d],
        )

    def ms_copy(d, c, late, landing=False):
        e = d if landing else d ^ 1
        tiles = pl.ds(3, 4) if late else pl.ds(0, 3)
        return remote(
            msg.at[d, c, tiles], rmsg.at[e, c, tiles],
            ms_send.at[d, c, late], ms_recv.at[e, c, late], around[d],
        )

    mg_copies = {
        2: remote(gr.at[0], gr.at[aggs], mg_send.at[0], mg_recv.at[1], around[2]),
        3: remote(gl.at[aggs], gl.at[0], mg_send.at[1], mg_recv.at[0], around[3]),
    }
    mg_landing = {
        2: remote(gl.at[aggs], gl.at[0], mg_send.at[0], mg_recv.at[0], around[2]),
        3: remote(gr.at[0], gr.at[aggs], mg_send.at[1], mg_recv.at[1], around[3]),
    }

    for behind in range(2):

        @pl.when(jnp.logical_and(slow == behind, there[behind]))
        def _():
            ps_copy(behind, 0).start()

    for d in range(4):

        @pl.when(there[d])
        def _():
            sp_copy(d).start()

    for behind in range(2):

        @pl.when(jnp.logical_and(slow == behind, there[behind]))
        def _():
            for c in order[1:]:
                ps_copy(behind, c).start()

    for d in (2, 3):

        @pl.when(there[d])
        def _():
            pg_copy(d).start()

    for behind in range(2):

        @pl.when(jnp.logical_and(slow == 1 - behind, there[behind]))
        def _():
            for c in order:
                ps_copy(behind, c).start()

    tile0 = jnp.zeros((B, 128), BF16)
    for d in range(4):

        @pl.when(jnp.logical_not(there[d]))
        def _():
            sp_h[d] = jnp.zeros((2, cols), jnp.int32)
            if d < 2:
                for y in range(cols):
                    pe[3 * d, 1 + y] = tile0
                for c in range(chunks):
                    for n in range(7):
                        rmsg[d, c, n] = tile0
            else:
                for r in range(2):
                    pe[1 + r, (cols + 1) * (d - 2)] = tile0
                for n in range(4):
                    if d == 2:
                        gl[0, n] = tile0
                    else:
                        gr[aggs, n] = tile0

    lo = lanes_low(16, BF16)
    hi = (1.0 - lanes_low(16, F32)).astype(BF16)
    low = lanes_low(B, F32) > 0.5

    def flag(condition, rows=16):
        return jnp.broadcast_to(jnp.where(condition, 1.0, 0.0).astype(F32), (rows, 128)).astype(BF16)

    reach = (flag(there[0]), flag(there[1]))
    side = (flag(there[2]), flag(there[3]))

    for g in range(aggs):
        for t in (0, 2, 10):
            out[0, g, :, 128 * t : 128 * t + 128] = tile0
        out[0, g, :, 1536:] = jnp.zeros((B, B), BF16)
        gs[g, 4, 0] = jnp.zeros((128, 128), BF16)
        gs[g, 3, 1] = jnp.zeros((128, 128), BF16)

    def masks_of_row(row, e):
        spill = spread(row, cols)
        straight = 1.0 - spill
        m0t[e, 1 : cols + 1] = straight if e in (0, 3) else straight * reach[e - 1][None]
        m1t[e, 2:cols] = spill[1 : cols - 1]
        m1t[e, 1] = spill[0] * side[0]
        m1t[e, cols] = spill[cols - 1] * side[1]

    own = sp_own[...].astype(F32)
    masks_of_row(own[0:1], 1)
    masks_of_row(own[1:2], 2)

    def prepare(t, carry):
        for r in range(2):
            pair = []
            for odd in range(2):
                y = 2 * t + odd
                tile = pe[1 + r, 1 + y]
                turn[r, y] = swap_halves(tile)
                pair.append(tile)
            flip[r, t] = below(pair).T
        return carry

    lax.fori_loop(0, aggs, prepare, 0)

    get_a.wait()

    def inner(r, y, odd):
        tile = turn[r, y]
        m0, m1 = m0t[1 + r, 1 + y], m1t[1 + r, 1 + y]
        first = tile * tall(m0 * lo)
        if odd == 0:
            return first, tile * tall(m1 * lo + hi), tile0
        return first, tile * tall(hi), tile * tall(m1 * lo)

    def keep(r, g):
        m0 = [m0t[1 + r, 1 + 2 * g + odd] for odd in range(2)]
        return flip[r, g, B:] * tall(m0[0] * lo + m0[1] * hi)

    def first_rows(r, c):
        values = []
        for i in range(2):
            g = 2 * c + i
            own = [inner(r, 2 * g + odd, odd) for odd in range(2)]
            for odd in range(2):
                y = 2 * g + odd
                first, second, third = inner(1 - r, y, odd)
                x_in = beside([tile0, second, third, first])
                at = y - 1 + 2 * odd
                tile = pe[1 + r, 1 + at]
                m0, m1 = m0t[1 + r, 1 + at], m1t[1 + r, 1 + at]
                if odd == 0:
                    y_out = beside([tile0, tile * tall(lo + m1 * hi), tile * tall(m0 * hi), tile0])
                else:
                    y_out = beside([tile * tall(m0 * hi), tile * tall(m1 * hi), tile * tall(lo), tile0])
                y_in = beside([*own[1 - odd], tile0])
                x_out = beside([tile0] * 4)
                blocks = [beside([*own[odd], tile0])]
                blocks += [x_out, x_in] if r == 0 else [x_in, x_out]
                blocks += [y_out, y_in] if odd == 0 else [y_in, y_out]
                left = a_v[r, y]
                value = jnp.dot(left[:, :256], below(blocks[:4]), preferred_element_type=F32)
                value += jnp.dot(left[:, 256:], blocks[4], preferred_element_type=F32)
                values.append(value)
        return values

    def first_step(c):
        values = [first_rows(r, c) for r in range(2)]
        leave = {}
        for r in range(2):
            for i in range(2):
                pair = below([v[:, 128:].astype(BF16) for v in values[r][2 * i : 2 * i + 2]])
                leave[r, i] = jnp.dot(keep(r, 2 * c + i), pair, preferred_element_type=F32)
        for r in range(2):
            for i in range(2):
                for odd in range(2):
                    value = values[r][2 * i + odd]
                    part[r, 4 * c + 2 * i + odd] = value[:, :384]
                    gs[2 * c + i, 1 - r, r, B * odd : B * odd + B] = value[:, 384:].astype(BF16)
                msg[r, c, i] = beside([leave[r, i][:, :B], leave[r, i][:, 128 : 128 + B]]).astype(BF16)
            msg[r, c, 2] = beside([leave[r, i][:, 256 : 256 + B] for i in range(2)]).astype(BF16)
        depart(c, 0)

    def last_rows(r, c):
        made = []
        for i in range(2):
            for odd in range(2):
                y = 4 * c + 2 * i + odd
                tile = pe[3 * r, 1 + y]
                m0, m1 = m0t[3 * r, 1 + y], m1t[3 * r, 1 + y]
                middle = tile * tall(m0 * hi)
                if odd == 0:
                    x_out = beside([tile * tall(lo), middle, tile * tall(m1 * hi)])
                else:
                    x_out = beside([tile * tall(lo + m1 * hi), middle, tile0])
                none = beside([tile0] * 3)
                left = a_v[r, y, :, :128] if r == 0 else a_v[r, y, :, 128:256]
                right = below([none, x_out] if r == 0 else [x_out, none])
                value = jnp.dot(left, right, preferred_element_type=F32)
                made.append((part[r, y] + value).astype(BF16))
        return made

    def last_step(c):
        for r in range(2):

            @pl.when(there[r])
            def _():
                ps_copy(r, c, True).wait_recv()

        made = [last_rows(r, c) for r in range(2)]
        leave = {}
        for r in range(2):
            for i in range(2):
                leave[r, i] = jnp.dot(
                    keep(r, 2 * c + i), below(made[r][2 * i : 2 * i + 2]), preferred_element_type=F32
                )
        for r in range(2):
            for i in range(2):
                for n, place in enumerate((r, 2, 3 + r)):
                    for odd in range(2):
                        gs[2 * c + i, place, r, B * odd : B * odd + B] = made[r][2 * i + odd][:, 128 * n : 128 * n + 128]
                msg[r, c, 3 + 2 * i] = leave[r, i][:, :128].astype(BF16)
                msg[r, c, 4 + 2 * i] = beside([leave[r, i][:, 128 + B : 256], leave[r, i][:, 256 + B :]]).astype(BF16)
        depart(c, 1)

    def depart(c, late):
        @pl.when(jnp.logical_and(slow == 1, there[1]))
        def _():
            ms_copy(1, c, late).start()

        @pl.when(there[0])
        def _():
            ms_copy(0, c, late).start()

        @pl.when(jnp.logical_and(slow == 0, there[1]))
        def _():
            ms_copy(1, c, late).start()

    def middle_step(c, carry):
        first_step(c)
        return carry

    lax.fori_loop(1, chunks - 1, middle_step, 0)

    for d in range(4):

        @pl.when(there[d])
        def _():
            sp_copy(d, True).wait_recv()

    masks_of_row(sp_h[0, 1:2].astype(F32), 0)
    masks_of_row(sp_h[1, 0:1].astype(F32), 3)
    for d, at, column in ((2, 0, cols - 1), (3, cols + 1, 0)):
        for r in range(2):
            spill = jnp.broadcast_to(sp_h[d, r : r + 1, column : column + 1].astype(F32), (16, 128)).astype(BF16)
            m0t[1 + r, at] = (1.0 - spill) * reach[r]
            m1t[1 + r, at] = spill

    for d in (2, 3):

        @pl.when(there[d])
        def _():
            pg_copy(d, True).wait_recv()

    def end_step(t, carry):
        first_step(t * (chunks - 1))
        return carry

    lax.fori_loop(0, 2, end_step, 0)


    def gather(g):
        right = beside([gs[g, n].reshape(256, 128) for n in range(5)])
        m1 = [[m1t[1 + r, 1 + 2 * g + odd] for odd in range(2)] for r in range(2)]
        left = below([
            beside([flip[r, g, :B] for r in range(2)]),
            beside([flip[r, g, B:] * tall(m1[r][0] * lo) for r in range(2)]),
            beside([flip[r, g, B:] * tall(m1[r][1] * hi) for r in range(2)]),
        ])
        return jnp.dot(left, right, preferred_element_type=F32)

    def spread_out(g, made):
        def piece(rows, n):
            return made[B * rows : B * rows + B, 128 * n : 128 * n + 128]

        um, up, ce, d0, d1 = (swap_halves(piece(0, n)) for n in range(5))
        acc[g, 0] = jnp.where(low, d0, um)
        acc[g, 1] = jnp.where(low, um, 0.0)
        acc[g, 2] = jnp.where(low, 0.0, ce)
        acc[g, 3] = jnp.where(low, ce, d0 + d1)
        acc[g, 4] = jnp.where(low, d1, up)
        acc[g, 5] = jnp.where(low, up, 0.0)
        um, up, ce, d0, d1 = (piece(1, n) for n in range(5))
        gr[g, 0] = jnp.where(low, um, d0).astype(BF16)
        gr[g, 1] = jnp.where(low, up, d1).astype(BF16)
        gr[g, 2] = ce.astype(BF16)
        gr[g, 3] = jnp.where(low, d0 + d1, 0.0).astype(BF16)
        um, up, ce, d0, d1 = (piece(2, n) for n in range(5))
        gl[g + 1, 0] = um.astype(BF16)
        gl[g + 1, 1] = up.astype(BF16)
        gl[g + 1, 2] = ce.astype(BF16)
        gl[g + 1, 3] = (d0 + d1).astype(BF16)

    def late_step(t, carry):
        last_step(jnp.where(t == 0, 0, jnp.where(t == 1, chunks - 1, t - 1)))
        for d, at in ((2, 0), (3, aggs - 1)):

            @pl.when(t == d - 2)
            def _():
                spread_out(at, gather(at))

                @pl.when(there[d])
                def _():
                    mg_copies[d].start()

        return carry

    lax.fori_loop(0, chunks, late_step, 0)

    def pair_step(t, carry):
        made = [gather(1 + 2 * t + i) for i in range(2)]
        for i in range(2):
            spread_out(1 + 2 * t + i, made[i])
        return carry

    lax.fori_loop(0, aggs // 2 - 1, pair_step, 0)
    for d in (2, 3):

        @pl.when(there[d])
        def _():
            mg_landing[d].wait_recv()

    def finish(t, carry):
        c = jnp.where(t == 0, 0, jnp.where(t == 1, chunks - 1, t - 1))
        for d in range(2):

            @pl.when(there[d])
            def _():
                for late in range(2):
                    ms_copy(d, c, late, True).wait_recv()

        for i in range(2):
            g = 2 * c + i
            be, bz, fe, fz = (rmsg[d, c, n].astype(F32) for d in range(2) for n in (i, 4 + 2 * i))
            b0, f0 = (rmsg[d, c, 3 + 2 * i].astype(F32) for d in range(2))
            b3, f3 = (rmsg[d, c, 2].astype(F32) for d in range(2))
            if i == 1:
                b3, f3 = swap_halves(b3), swap_halves(f3)
            b1, f1 = jnp.where(low, be, swap_halves(bz)), jnp.where(low, fe, swap_halves(fz))
            b2, f2 = jnp.where(low, swap_halves(be), bz), jnp.where(low, swap_halves(fe), fz)
            l0, l1, l2, l3 = (gl[g, n].astype(F32) for n in range(4))
            r0, r1, r2, r3 = (gr[g + 1, n].astype(F32) for n in range(4))
            tiles = (
                (1, jnp.where(low, b3, 0.0)),
                (3, acc[g, 0] + b1 + l0 + jnp.where(low, 0.0, r0)),
                (4, acc[g, 1] + jnp.where(low, b2 + r0, 0.0)),
                (5, acc[g, 2] + l2 + jnp.where(low, 0.0, b2 + f2)),
                (6, acc[g, 3] + b0 + f0 + l3 + r2),
                (7, r3),
                (8, acc[g, 4] + f1 + l1 + jnp.where(low, 0.0, r1)),
                (9, acc[g, 5] + jnp.where(low, f2 + r1, 0.0)),
                (11, jnp.where(low, f3, 0.0)),
            )
            for t, value in tiles:
                out[0, g, :, 128 * t : 128 * t + 128] = value.astype(BF16)
        return carry

    lax.fori_loop(0, chunks, finish, 0)

    for d in range(4):

        @pl.when(there[d])
        def _():
            sp_copy(d).wait_send()
            if d < 2:
                for c in range(chunks):
                    ps_copy(d, c).wait_send()
                    for late in range(2):
                        ms_copy(d, c, late).wait_send()
            else:
                pg_copy(d).wait_send()
                mg_copies[d].wait_send()


def local(a_vals, p_vals, spill_axis):
    n_sub = lax.axis_size("sub")
    n_gy = lax.axis_size("gy")
    cols = a_vals.shape[1]
    aggs = cols // 2
    chunks = aggs // 2
    dma = pltpu.SemaphoreType.DMA
    return pl.pallas_call(
        functools.partial(kernel, n_sub, n_gy, cols),
        out_shape=jax.ShapeDtypeStruct((1, aggs, B, SLOTS * B), BF16),
        in_specs=[pl.BlockSpec(memory_space=pl.ANY)] * 3,
        out_specs=pl.BlockSpec(memory_space=pltpu.VMEM),
        scratch_shapes=[
            pltpu.VMEM((2, cols, B, 5 * B), BF16),
            pltpu.VMEM((4, cols + 2, B, 128), BF16),
            pltpu.VMEM((2, cols), jnp.int32),
            pltpu.VMEM((4, 2, cols), jnp.int32),
            pltpu.VMEM((4, cols + 2, 16, 128), BF16),
            pltpu.VMEM((4, cols + 2, 16, 128), BF16),
            pltpu.VMEM((2, cols, B, 128), BF16),
            pltpu.VMEM((2, aggs, 128, 128), BF16),
            pltpu.VMEM((2, cols, B, 384), F32),
            pltpu.VMEM((aggs, 5, 2, 128, 128), BF16),
            pltpu.VMEM((2, chunks, 7, B, 128), BF16),
            pltpu.VMEM((2, chunks, 7, B, 128), BF16),
            pltpu.VMEM((aggs, 6, B, 128), F32),
            pltpu.VMEM((aggs + 1, 4, B, 128), BF16),
            pltpu.VMEM((aggs + 1, 4, B, 128), BF16),
            dma((3,)),
            dma((4,)),
            dma((4,)),
            dma((2, chunks)),
            dma((2, chunks)),
            dma((2,)),
            dma((2,)),
            dma((2, chunks, 2)),
            dma((2, chunks, 2)),
            dma((2,)),
            dma((2,)),
        ],
        compiler_params=pltpu.CompilerParams(
            collective_id=0, has_side_effects=True, vmem_limit_bytes=40 * 1024 * 1024
        ),
        cost_estimate=pl.CostEstimate(flops=1_300_000_000, bytes_accessed=4_000_000, transcendentals=0),
    )(*(pltpu.with_memory_space_constraint(x, pltpu.HBM) for x in (a_vals, p_vals, spill_axis)))


def solution(mesh):
    return jax.shard_map(
        local,
        mesh=mesh,
        in_specs=(P("sub", "gy", None, None), P("sub", "gy", None, None), P("sub", "gy")),
        out_specs=P("sub", "gy", None, None),
        check_vma=False,
    )
```

```python
import functools

import jax
import jax.numpy as jnp
from jax import lax
from jax.experimental import pallas as pl
from jax.experimental.pallas import tpu as pltpu
from jax.sharding import PartitionSpec as P

MESH = pl.DeviceIdType.MESH
F32 = jnp.float32
BF16 = jnp.bfloat16
B = 64
SLOTS = 25


def lanes_low(rows, dtype):
    lane = lax.broadcasted_iota(jnp.int32, (rows, 128), 1)
    return jnp.where(lane < B, 1.0, 0.0).astype(dtype)


def swap_halves(tile):
    return jnp.concatenate([tile[:, B:], tile[:, :B]], axis=1)


def tall(mask):
    return jnp.concatenate([mask] * 4, axis=0)


def spread(row, cols):
    wide = jnp.broadcast_to(row, (cols, cols))
    at = lax.broadcasted_iota(jnp.int32, (cols, cols), 0)
    lane = lax.broadcasted_iota(jnp.int32, (cols, cols), 1)
    column = jnp.sum(jnp.where(at == lane, wide, 0.0), axis=1, keepdims=True)
    column = jnp.broadcast_to(column, (cols, 128))
    return jnp.broadcast_to(column[:, None, :], (cols, 16, 128)).astype(BF16)


def beside(tiles):
    return jnp.concatenate(tiles, axis=1)


def below(tiles):
    return jnp.concatenate(tiles, axis=0)


def kernel(
    n_sub, n_gy, cols,
    a_hbm, p_hbm, sp_hbm, out,
    a_v, pe, sp_own, sp_h, m0t, m1t, turn, flip, part, facing, msg, rmsg, acc, gl, gr,
    local_sem, sp_send, sp_recv, ps_send, ps_recv, pg_send, pg_recv,
    ms_send, ms_recv, mg_send, mg_recv,
):
    s = lax.axis_index("sub")
    z = lax.axis_index("gy")
    aggs = cols // 2
    chunks = aggs // 2
    around = (
        (lax.rem(s + n_sub - 1, n_sub), z),
        (lax.rem(s + 1, n_sub), z),
        (s, lax.rem(z + n_gy - 1, n_gy)),
        (s, lax.rem(z + 1, n_gy)),
    )
    there = (s > 0, s < n_sub - 1, z > 0, z < n_gy - 1)
    slow = lax.rem(s, 2)
    order = [0, chunks - 1, *range(1, chunks - 1)]

    barrier = pltpu.get_barrier_semaphore()
    for d in range(4):

        @pl.when(there[d])
        def _():
            pl.semaphore_signal(barrier, inc=1, device_id=around[d], device_id_type=MESH)

    get_sp = pltpu.make_async_copy(sp_hbm, sp_own, local_sem.at[0])
    get_p = pltpu.make_async_copy(p_hbm, pe.at[1:3, 1 : cols + 1], local_sem.at[1])
    get_a = pltpu.make_async_copy(a_hbm, a_v, local_sem.at[2])
    get_sp.start()
    get_p.start()
    get_a.start()
    def remote(src, dst, send, recv, device):
        return pltpu.make_async_remote_copy(
            src_ref=src, dst_ref=dst, send_sem=send, recv_sem=recv, device_id=device, device_id_type=MESH
        )

    def sp_copy(d, landing=False):
        e = d if landing else d ^ 1
        return remote(sp_own, sp_h.at[e], sp_send.at[d], sp_recv.at[e], around[d])

    def pg_copy(d, landing=False):
        e = d if landing else d ^ 1
        return remote(
            pe.at[1:3, 1 + (cols - 1) * (d - 2)], pe.at[1:3, (cols + 1) * (e - 2)],
            pg_send.at[d - 2], pg_recv.at[e - 2], around[d],
        )

    def ps_copy(d, c, landing=False):
        e = d if landing else d ^ 1
        return remote(
            pe.at[1 + d, pl.ds(1 + 4 * c, 4)], pe.at[3 * e, pl.ds(1 + 4 * c, 4)],
            ps_send.at[d, c], ps_recv.at[e, c], around[d],
        )

    def ms_copy(d, c, late, landing=False):
        e = d if landing else d ^ 1
        tiles = pl.ds(3, 4) if late else pl.ds(0, 3)
        return remote(
            msg.at[d, c, tiles], rmsg.at[e, c, tiles],
            ms_send.at[d, c, late], ms_recv.at[e, c, late], around[d],
        )

    mg_copies = {
        2: remote(gr.at[0], gr.at[aggs], mg_send.at[0], mg_recv.at[1], around[2]),
        3: remote(gl.at[aggs], gl.at[0], mg_send.at[1], mg_recv.at[0], around[3]),
    }
    mg_landing = {
        2: remote(gl.at[aggs], gl.at[0], mg_send.at[0], mg_recv.at[0], around[2]),
        3: remote(gr.at[0], gr.at[aggs], mg_send.at[1], mg_recv.at[1], around[3]),
    }

    tile0 = jnp.zeros((B, 128), BF16)
    for d in range(4):

        @pl.when(jnp.logical_not(there[d]))
        def _():
            sp_h[d] = jnp.zeros((2, cols), jnp.int32)
            if d < 2:
                for y in range(cols):
                    pe[3 * d, 1 + y] = tile0
                for c in range(chunks):
                    for n in range(7):
                        rmsg[d, c, n] = tile0
            else:
                for r in range(2):
                    pe[1 + r, (cols + 1) * (d - 2)] = tile0
                for n in range(4):
                    if d == 2:
                        gl[0, n] = tile0
                    else:
                        gr[aggs, n] = tile0

    lo = lanes_low(16, BF16)
    hi = (1.0 - lanes_low(16, F32)).astype(BF16)
    low = lanes_low(B, F32) > 0.5

    def flag(condition, rows=16):
        return jnp.broadcast_to(jnp.where(condition, 1.0, 0.0).astype(F32), (rows, 128)).astype(BF16)

    reach = (flag(there[0]), flag(there[1]))
    side = (flag(there[2]), flag(there[3]))

    for g in range(aggs):
        for t in (0, 2, 10):
            out[0, g, :, 128 * t : 128 * t + 128] = tile0
        out[0, g, :, 1536:] = jnp.zeros((B, B), BF16)

    def masks_of_row(row, e):
        spill = spread(row, cols)
        straight = 1.0 - spill
        m0t[e, 1 : cols + 1] = straight if e in (0, 3) else straight * reach[e - 1][None]
        m1t[e, 2:cols] = spill[1 : cols - 1]
        m1t[e, 1] = spill[0] * side[0]
        m1t[e, cols] = spill[cols - 1] * side[1]

    get_sp.wait()
    own = sp_own[...].astype(F32)
    masks_of_row(own[0:1], 1)
    masks_of_row(own[1:2], 2)
    get_p.wait()
    ones = [jnp.where(t, 1, 0).astype(jnp.int32) for t in there]
    pl.semaphore_wait(barrier, ones[0] + ones[1] + ones[2] + ones[3])

    for d in range(4):

        @pl.when(there[d])
        def _():
            sp_copy(d).start()
            if d > 1:
                pg_copy(d).start()

    for behind in range(2):

        @pl.when(jnp.logical_and(slow == behind, there[behind]))
        def _():
            for c in order:
                ps_copy(behind, c).start()

    for behind in range(2):

        @pl.when(jnp.logical_and(slow == 1 - behind, there[behind]))
        def _():
            for c in order:
                ps_copy(behind, c).start()


    def prepare(t, carry):
        for r in range(2):
            pair = []
            for odd in range(2):
                y = 2 * t + odd
                tile = pe[1 + r, 1 + y]
                turn[r, y] = swap_halves(tile)
                pair.append(tile)
            flip[r, t] = below(pair).T
        return carry

    lax.fori_loop(0, aggs, prepare, 0)

    get_a.wait()

    def inner(r, y, odd):
        tile = turn[r, y]
        m0, m1 = m0t[1 + r, 1 + y], m1t[1 + r, 1 + y]
        first = tile * tall(m0 * lo)
        if odd == 0:
            return first, tile * tall(m1 * lo + hi), tile0
        return first, tile * tall(hi), tile * tall(m1 * lo)

    def spills(r, g):
        return [(m0t[1 + r, 1 + 2 * g + odd], m1t[1 + r, 1 + 2 * g + odd]) for odd in range(2)]

    half0 = jnp.zeros((B, B), BF16)

    def leaving(r, g):
        (m0e, _), (m0o, _) = spills(r, g)
        return flip[r, g, B:] * tall(m0e * lo + m0o * hi)

    def staying(r, g):
        (_, m1e), (_, m1o) = spills(r, g)
        second = flip[r, g, B:]
        return below([flip[r, g, :B], second * tall(m1e * lo), second * tall(m1o * hi)])

    def operator(r, g):
        even, odd = a_v[r, 2 * g], a_v[r, 2 * g + 1]
        return below([
            beside([even, half0, tile0]),
            beside([odd[:, 192:256], half0, tile0, odd[:, :128], odd[:, 128:192], odd[:, 256:]]),
        ])

    def outside(r, g):
        blocks = []
        for odd in range(2):
            y = 2 * g + odd
            tile = pe[3 * r, 1 + y]
            m0, m1 = m0t[3 * r, 1 + y], m1t[3 * r, 1 + y]
            middle = tile * tall(m0 * hi)
            if odd == 0:
                blocks.append(beside([tile * tall(lo), middle, tile * tall(m1 * hi)]))
            else:
                blocks.append(beside([tile * tall(lo + m1 * hi), middle, tile0]))
        return blocks

    def columns(r, g, halo):
        into = []
        for odd in range(2):
            first, second, third = inner(1 - r, 2 * g + odd, odd)
            into.append(beside([tile0, second, third, first]))
        out = [beside([b, tile0]) for b in outside(r, g)] if halo else [beside([tile0] * 4)] * 2
        minus, plus = (out, into) if r == 0 else (into, out)
        own = [beside([*inner(r, 2 * g + odd, odd), tile0]) for odd in range(2)]
        tile = pe[1 + r, 2 * g]
        m0, m1 = m0t[1 + r, 2 * g], m1t[1 + r, 2 * g]
        prior = beside([tile0, tile * tall(lo + m1 * hi), tile * tall(m0 * hi), tile0])
        tile = pe[1 + r, 2 * g + 3]
        m0, m1 = m0t[1 + r, 2 * g + 3], m1t[1 + r, 2 * g + 3]
        following = beside([tile * tall(m0 * hi), tile * tall(m1 * hi), tile * tall(lo), tile0])
        return below([own[0], minus[0], plus[0], prior, own[1], minus[1], plus[1], following])

    units = [(r, i) for i in range(2) for r in range(2)]

    def first_step(some):
        value, leave = {}, {}
        every = [(r, 2 * c + i) for c in some for r, i in units]
        for r, g in every:
            value[r, g] = jnp.dot(leaving(r, g), operator(r, g), preferred_element_type=F32).astype(BF16)
        for r, g in every:
            leave[r, g] = jnp.dot(value[r, g], columns(r, g, False), preferred_element_type=F32)
        for r, g in every:
            kept, sent = value[r, g], leave[r, g]
            facing[r, g] = beside([kept[:, 128 * n : 128 * n + 128] for n in (r, 2 + r)])
            part[r, g] = sent[:, :384]
            msg[r, g // 2, g % 2] = beside([sent[:, 128 : 128 + B], sent[:, 256 : 256 + B]]).astype(BF16)
        for c in some:
            for r in range(2):
                msg[r, c, 2] = beside([leave[r, 2 * c + i][:, 384 : 384 + B] for i in range(2)]).astype(BF16)
            depart(c, 0)

    def last_step(c):
        for r in range(2):

            @pl.when(there[r])
            def _():
                ps_copy(r, c, True).wait_recv()

        leave = {}
        none = beside([tile0] * 3)
        for r, i in units:
            even, odd = outside(r, 2 * c + i)
            right = below([none, even, none, odd] if r == 0 else [even, none, odd, none])
            leave[r, i] = jnp.dot(facing[r, 2 * c + i], right, preferred_element_type=F32)
        for r, i in units:
            sent = part[r, 2 * c + i] + leave[r, i]
            msg[r, c, 3 + 2 * i] = sent[:, :128].astype(BF16)
            msg[r, c, 4 + 2 * i] = beside([sent[:, 128 + B : 256], sent[:, 256 + B :]]).astype(BF16)
        depart(c, 1)

    def own_step(some):
        value, made = {}, {}
        every = [(r, g) for g in some for r in range(2)]
        for r, g in every:
            value[r, g] = jnp.dot(staying(r, g), operator(r, g), preferred_element_type=F32).astype(BF16)
        for r, g in every:
            made[r, g] = jnp.dot(value[r, g], columns(r, g, True), preferred_element_type=F32)
        for g in some:
            spread_out(g, made[0, g], made[1, g])

    def depart(c, late):
        @pl.when(jnp.logical_and(slow == 1, there[1]))
        def _():
            ms_copy(1, c, late).start()

        @pl.when(there[0])
        def _():
            ms_copy(0, c, late).start()

        @pl.when(jnp.logical_and(slow == 0, there[1]))
        def _():
            ms_copy(1, c, late).start()

    ends, middle = [0, chunks - 1], list(range(1, chunks - 1))
    if middle:
        first_step(middle)

    for d in (2, 3):

        @pl.when(there[d])
        def _():
            sp_copy(d, True).wait_recv()

    for d, at, column in ((2, 0, cols - 1), (3, cols + 1, 0)):
        for r in range(2):
            spill = jnp.broadcast_to(sp_h[d, r : r + 1, column : column + 1].astype(F32), (16, 128)).astype(BF16)
            m0t[1 + r, at] = (1.0 - spill) * reach[r]
            m1t[1 + r, at] = spill

    for d in (2, 3):

        @pl.when(there[d])
        def _():
            pg_copy(d, True).wait_recv()

    first_step(ends)
    for d in (0, 1):

        @pl.when(there[d])
        def _():
            sp_copy(d, True).wait_recv()

    masks_of_row(sp_h[0, 1:2].astype(F32), 0)
    masks_of_row(sp_h[1, 0:1].astype(F32), 3)


    def spread_out(g, before, after):
        def tiles(rows):
            b, a = (
                [x[B * rows : B * rows + B, 128 * n : 128 * n + 128] for n in range(4)] for x in (before, after)
            )
            return b[0] + a[3], a[0] + b[3], b[1] + a[1], b[2], a[2]

        um, up, ce, d0, d1 = (swap_halves(x) for x in tiles(0))
        acc[g, 0] = jnp.where(low, d0, um)
        acc[g, 1] = jnp.where(low, um, 0.0)
        acc[g, 2] = jnp.where(low, 0.0, ce)
        acc[g, 3] = jnp.where(low, ce, d0 + d1)
        acc[g, 4] = jnp.where(low, d1, up)
        acc[g, 5] = jnp.where(low, up, 0.0)
        um, up, ce, d0, d1 = tiles(1)
        gr[g, 0] = jnp.where(low, um, d0).astype(BF16)
        gr[g, 1] = jnp.where(low, up, d1).astype(BF16)
        gr[g, 2] = ce.astype(BF16)
        gr[g, 3] = jnp.where(low, d0 + d1, 0.0).astype(BF16)
        um, up, ce, d0, d1 = tiles(2)
        gl[g + 1, 0] = um.astype(BF16)
        gl[g + 1, 1] = up.astype(BF16)
        gl[g + 1, 2] = ce.astype(BF16)
        gl[g + 1, 3] = (d0 + d1).astype(BF16)

    def nth(t):
        return jnp.where(t == 0, 0, jnp.where(t == 1, chunks - 1, t - 1))

    def late_step(t, carry):
        last_step(nth(t))
        return carry

    lax.fori_loop(0, 2, late_step, 0)
    own_step([0, aggs - 1])
    for d in (2, 3):

        @pl.when(there[d])
        def _():
            mg_copies[d].start()

    lax.fori_loop(2, chunks, late_step, 0)
    inner_aggs = list(range(1, aggs - 1))
    for first in range(0, aggs - 2, 3):
        own_step(inner_aggs[first : first + 3])
    for d in (2, 3):

        @pl.when(there[d])
        def _():
            mg_landing[d].wait_recv()

    def finish(t, carry):
        c = nth(t)
        for d in range(2):

            @pl.when(there[d])
            def _():
                for late in range(2):
                    ms_copy(d, c, late, True).wait_recv()

        for i in range(2):
            g = 2 * c + i
            be, bz, fe, fz = (rmsg[d, c, n].astype(F32) for d in range(2) for n in (i, 4 + 2 * i))
            b0, f0 = (rmsg[d, c, 3 + 2 * i].astype(F32) for d in range(2))
            b3, f3 = (rmsg[d, c, 2].astype(F32) for d in range(2))
            if i == 1:
                b3, f3 = swap_halves(b3), swap_halves(f3)
            b1, f1 = jnp.where(low, be, swap_halves(bz)), jnp.where(low, fe, swap_halves(fz))
            b2, f2 = jnp.where(low, swap_halves(be), bz), jnp.where(low, swap_halves(fe), fz)
            l0, l1, l2, l3 = (gl[g, n].astype(F32) for n in range(4))
            r0, r1, r2, r3 = (gr[g + 1, n].astype(F32) for n in range(4))
            tiles = (
                (1, jnp.where(low, b3, 0.0)),
                (3, acc[g, 0] + b1 + l0 + jnp.where(low, 0.0, r0)),
                (4, acc[g, 1] + jnp.where(low, b2 + r0, 0.0)),
                (5, acc[g, 2] + l2 + jnp.where(low, 0.0, b2 + f2)),
                (6, acc[g, 3] + b0 + f0 + l3 + r2),
                (7, r3),
                (8, acc[g, 4] + f1 + l1 + jnp.where(low, 0.0, r1)),
                (9, acc[g, 5] + jnp.where(low, f2 + r1, 0.0)),
                (11, jnp.where(low, f3, 0.0)),
            )
            for t, value in tiles:
                out[0, g, :, 128 * t : 128 * t + 128] = value.astype(BF16)
        return carry

    lax.fori_loop(0, chunks, finish, 0)

    for d in range(4):

        @pl.when(there[d])
        def _():
            sp_copy(d).wait_send()
            if d < 2:
                for c in range(chunks):
                    ps_copy(d, c).wait_send()
                    for late in range(2):
                        ms_copy(d, c, late).wait_send()
            else:
                pg_copy(d).wait_send()
                mg_copies[d].wait_send()


def local(a_vals, p_vals, spill_axis):
    n_sub = lax.axis_size("sub")
    n_gy = lax.axis_size("gy")
    cols = a_vals.shape[1]
    aggs = cols // 2
    chunks = aggs // 2
    dma = pltpu.SemaphoreType.DMA
    return pl.pallas_call(
        functools.partial(kernel, n_sub, n_gy, cols),
        out_shape=jax.ShapeDtypeStruct((1, aggs, B, SLOTS * B), BF16),
        in_specs=[pl.BlockSpec(memory_space=pl.ANY)] * 3,
        out_specs=pl.BlockSpec(memory_space=pltpu.VMEM),
        scratch_shapes=[
            pltpu.VMEM((2, cols, B, 5 * B), BF16),
            pltpu.VMEM((4, cols + 2, B, 128), BF16),
            pltpu.VMEM((2, cols), jnp.int32),
            pltpu.VMEM((4, 2, cols), jnp.int32),
            pltpu.VMEM((4, cols + 2, 16, 128), BF16),
            pltpu.VMEM((4, cols + 2, 16, 128), BF16),
            pltpu.VMEM((2, cols, B, 128), BF16),
            pltpu.VMEM((2, aggs, 128, 128), BF16),
            pltpu.VMEM((2, aggs, B, 384), F32),
            pltpu.VMEM((2, aggs, B, 256), BF16),
            pltpu.VMEM((2, chunks, 7, B, 128), BF16),
            pltpu.VMEM((2, chunks, 7, B, 128), BF16),
            pltpu.VMEM((aggs, 6, B, 128), F32),
            pltpu.VMEM((aggs + 1, 4, B, 128), BF16),
            pltpu.VMEM((aggs + 1, 4, B, 128), BF16),
            dma((3,)),
            dma((4,)),
            dma((4,)),
            dma((2, chunks)),
            dma((2, chunks)),
            dma((2,)),
            dma((2,)),
            dma((2, chunks, 2)),
            dma((2, chunks, 2)),
            dma((2,)),
            dma((2,)),
        ],
        compiler_params=pltpu.CompilerParams(
            collective_id=0, has_side_effects=True, vmem_limit_bytes=40 * 1024 * 1024
        ),
        cost_estimate=pl.CostEstimate(flops=1_300_000_000, bytes_accessed=4_000_000, transcendentals=0),
    )(*(pltpu.with_memory_space_constraint(x, pltpu.HBM) for x in (a_vals, p_vals, spill_axis)))


def solution(mesh):
    return jax.shard_map(
        local,
        mesh=mesh,
        in_specs=(P("sub", "gy", None, None), P("sub", "gy", None, None), P("sub", "gy")),
        out_specs=P("sub", "gy", None, None),
        check_vma=False,
    )
```

```python
import functools

import jax
import jax.numpy as jnp
from jax import lax
from jax.experimental import pallas as pl
from jax.experimental.pallas import tpu as pltpu
from jax.sharding import PartitionSpec as P

MESH = pl.DeviceIdType.MESH
F32 = jnp.float32
BF16 = jnp.bfloat16
B = 64
SLOTS = 25


def lanes_low(rows, dtype):
    lane = lax.broadcasted_iota(jnp.int32, (rows, 128), 1)
    return jnp.where(lane < B, 1.0, 0.0).astype(dtype)


def swap_halves(tile):
    return jnp.concatenate([tile[:, B:], tile[:, :B]], axis=1)


def tall(mask):
    return jnp.concatenate([mask] * 4, axis=0)


def spread(row, cols):
    wide = jnp.broadcast_to(row, (cols, cols))
    at = lax.broadcasted_iota(jnp.int32, (cols, cols), 0)
    lane = lax.broadcasted_iota(jnp.int32, (cols, cols), 1)
    column = jnp.sum(jnp.where(at == lane, wide, 0.0), axis=1, keepdims=True)
    column = jnp.broadcast_to(column, (cols, 128))
    return jnp.broadcast_to(column[:, None, :], (cols, 16, 128)).astype(BF16)


def beside(tiles):
    return jnp.concatenate(tiles, axis=1)


def below(tiles):
    return jnp.concatenate(tiles, axis=0)


def kernel(
    n_sub, n_gy, cols,
    a_hbm, p_hbm, sp_hbm, out,
    a_v, pe, sp_own, sp_h, m0t, m1t, turn, flip, part, facing, msg, rmsg, acc, gl, gr,
    local_sem, sp_send, sp_recv, ps_send, ps_recv, pg_send, pg_recv,
    ms_send, ms_recv, mg_send, mg_recv,
):
    s = lax.axis_index("sub")
    z = lax.axis_index("gy")
    aggs = cols // 2
    chunks = aggs // 2
    around = (
        (lax.rem(s + n_sub - 1, n_sub), z),
        (lax.rem(s + 1, n_sub), z),
        (s, lax.rem(z + n_gy - 1, n_gy)),
        (s, lax.rem(z + 1, n_gy)),
    )
    there = (s > 0, s < n_sub - 1, z > 0, z < n_gy - 1)
    slow = lax.rem(s, 2)
    order = [0, chunks - 1, *range(1, chunks - 1)]

    barrier = pltpu.get_barrier_semaphore()
    for d in range(4):

        @pl.when(there[d])
        def _():
            pl.semaphore_signal(barrier, inc=1, device_id=around[d], device_id_type=MESH)

    get_sp = pltpu.make_async_copy(sp_hbm, sp_own, local_sem.at[0])
    get_p = pltpu.make_async_copy(p_hbm, pe.at[1:3, 1 : cols + 1], local_sem.at[1])
    get_a = pltpu.make_async_copy(a_hbm, a_v, local_sem.at[2])
    get_sp.start()
    get_p.start()
    get_a.start()
    def remote(src, dst, send, recv, device):
        return pltpu.make_async_remote_copy(
            src_ref=src, dst_ref=dst, send_sem=send, recv_sem=recv, device_id=device, device_id_type=MESH
        )

    def sp_copy(d, landing=False):
        e = d if landing else d ^ 1
        return remote(sp_own, sp_h.at[e], sp_send.at[d], sp_recv.at[e], around[d])

    def pg_copy(d, landing=False):
        e = d if landing else d ^ 1
        return remote(
            pe.at[1:3, 1 + (cols - 1) * (d - 2)], pe.at[1:3, (cols + 1) * (e - 2)],
            pg_send.at[d - 2], pg_recv.at[e - 2], around[d],
        )

    def ps_copy(d, c, landing=False):
        e = d if landing else d ^ 1
        return remote(
            pe.at[1 + d, pl.ds(1 + 4 * c, 4)], pe.at[3 * e, pl.ds(1 + 4 * c, 4)],
            ps_send.at[d, c], ps_recv.at[e, c], around[d],
        )

    def ms_copy(d, c, late, landing=False):
        e = d if landing else d ^ 1
        tiles = pl.ds(3, 4) if late else pl.ds(0, 3)
        return remote(
            msg.at[d, c, tiles], rmsg.at[e, c, tiles],
            ms_send.at[d, c, late], ms_recv.at[e, c, late], around[d],
        )

    mg_copies = {
        2: remote(gr.at[0], gr.at[aggs], mg_send.at[0], mg_recv.at[1], around[2]),
        3: remote(gl.at[aggs], gl.at[0], mg_send.at[1], mg_recv.at[0], around[3]),
    }
    mg_landing = {
        2: remote(gl.at[aggs], gl.at[0], mg_send.at[0], mg_recv.at[0], around[2]),
        3: remote(gr.at[0], gr.at[aggs], mg_send.at[1], mg_recv.at[1], around[3]),
    }

    tile0 = jnp.zeros((B, 128), BF16)
    for d in range(4):

        @pl.when(jnp.logical_not(there[d]))
        def _():
            sp_h[d] = jnp.zeros((2, cols), jnp.int32)
            if d < 2:
                for y in range(cols):
                    pe[3 * d, 1 + y] = tile0
                for c in range(chunks):
                    for n in range(7):
                        rmsg[d, c, n] = tile0
            else:
                for r in range(2):
                    pe[1 + r, (cols + 1) * (d - 2)] = tile0
                for n in range(4):
                    if d == 2:
                        gl[0, n] = tile0
                    else:
                        gr[aggs, n] = tile0

    lo = lanes_low(16, BF16)
    hi = (1.0 - lanes_low(16, F32)).astype(BF16)
    low = lanes_low(B, F32) > 0.5

    def flag(condition, rows=16):
        return jnp.broadcast_to(jnp.where(condition, 1.0, 0.0).astype(F32), (rows, 128)).astype(BF16)

    reach = (flag(there[0]), flag(there[1]))
    side = (flag(there[2]), flag(there[3]))

    for g in range(aggs):
        for t in (0, 2, 10):
            out[0, g, :, 128 * t : 128 * t + 128] = tile0
        out[0, g, :, 1536:] = jnp.zeros((B, B), BF16)

    def masks_of_row(row, e):
        spill = spread(row, cols)
        straight = 1.0 - spill
        m0t[e, 1 : cols + 1] = straight if e in (0, 3) else straight * reach[e - 1][None]
        m1t[e, 2:cols] = spill[1 : cols - 1]
        m1t[e, 1] = spill[0] * side[0]
        m1t[e, cols] = spill[cols - 1] * side[1]

    get_sp.wait()
    own = sp_own[...].astype(F32)
    masks_of_row(own[0:1], 1)
    masks_of_row(own[1:2], 2)
    get_p.wait()
    ones = [jnp.where(t, 1, 0).astype(jnp.int32) for t in there]
    pl.semaphore_wait(barrier, ones[0] + ones[1] + ones[2] + ones[3])

    for behind in range(2):

        @pl.when(jnp.logical_and(slow == behind, there[behind]))
        def _():
            ps_copy(behind, 0).start()

    for d in (2, 3, 0, 1):

        @pl.when(there[d])
        def _():
            sp_copy(d).start()
            if d > 1:
                pg_copy(d).start()

    for behind in range(2):

        @pl.when(jnp.logical_and(slow == behind, there[behind]))
        def _():
            for c in order[1:]:
                ps_copy(behind, c).start()

    for behind in range(2):

        @pl.when(jnp.logical_and(slow == 1 - behind, there[behind]))
        def _():
            for c in order:
                ps_copy(behind, c).start()


    def prepare(t, carry):
        for r in range(2):
            pair = []
            for odd in range(2):
                y = 2 * t + odd
                tile = pe[1 + r, 1 + y]
                turn[r, y] = swap_halves(tile)
                pair.append(tile)
            flip[r, t] = below(pair).T
        return carry

    lax.fori_loop(0, aggs, prepare, 0)

    get_a.wait()

    def inner(r, y, odd):
        tile = turn[r, y]
        m0, m1 = m0t[1 + r, 1 + y], m1t[1 + r, 1 + y]
        first = tile * tall(m0 * lo)
        if odd == 0:
            return first, tile * tall(m1 * lo + hi), tile0
        return first, tile * tall(hi), tile * tall(m1 * lo)

    def spills(r, g):
        return [(m0t[1 + r, 1 + 2 * g + odd], m1t[1 + r, 1 + 2 * g + odd]) for odd in range(2)]

    half0 = jnp.zeros((B, B), BF16)

    def leaving(r, g):
        (m0e, _), (m0o, _) = spills(r, g)
        return flip[r, g, B:] * tall(m0e * lo + m0o * hi)

    def staying(r, g):
        (_, m1e), (_, m1o) = spills(r, g)
        second = flip[r, g, B:]
        return below([flip[r, g, :B], second * tall(m1e * lo), second * tall(m1o * hi)])

    def operator(r, g):
        even, odd = a_v[r, 2 * g], a_v[r, 2 * g + 1]
        return below([
            beside([even, half0, tile0]),
            beside([odd[:, 192:256], half0, tile0, odd[:, :128], odd[:, 128:192], odd[:, 256:]]),
        ])

    def outside(r, g):
        blocks = []
        for odd in range(2):
            y = 2 * g + odd
            tile = pe[3 * r, 1 + y]
            m0, m1 = m0t[3 * r, 1 + y], m1t[3 * r, 1 + y]
            middle = tile * tall(m0 * hi)
            if odd == 0:
                blocks.append(beside([tile * tall(lo), middle, tile * tall(m1 * hi)]))
            else:
                blocks.append(beside([tile * tall(lo + m1 * hi), middle, tile0]))
        return blocks

    def columns(r, g, halo):
        into = []
        for odd in range(2):
            first, second, third = inner(1 - r, 2 * g + odd, odd)
            into.append(beside([tile0, second, third, first]))
        out = [beside([b, tile0]) for b in outside(r, g)] if halo else [beside([tile0] * 4)] * 2
        minus, plus = (out, into) if r == 0 else (into, out)
        own = [beside([*inner(r, 2 * g + odd, odd), tile0]) for odd in range(2)]
        tile = pe[1 + r, 2 * g]
        m0, m1 = m0t[1 + r, 2 * g], m1t[1 + r, 2 * g]
        prior = beside([tile0, tile * tall(lo + m1 * hi), tile * tall(m0 * hi), tile0])
        tile = pe[1 + r, 2 * g + 3]
        m0, m1 = m0t[1 + r, 2 * g + 3], m1t[1 + r, 2 * g + 3]
        following = beside([tile * tall(m0 * hi), tile * tall(m1 * hi), tile * tall(lo), tile0])
        return below([own[0], minus[0], plus[0], prior, own[1], minus[1], plus[1], following])

    units = [(r, i) for i in range(2) for r in range(2)]

    def first_step(some):
        value, leave = {}, {}
        every = [(r, 2 * c + i) for c in some for r, i in units]
        for r, g in every:
            value[r, g] = jnp.dot(leaving(r, g), operator(r, g), preferred_element_type=F32).astype(BF16)
        for r, g in every:
            leave[r, g] = jnp.dot(value[r, g], columns(r, g, False), preferred_element_type=F32)
        for r, g in every:
            kept, sent = value[r, g], leave[r, g]
            facing[r, g] = beside([kept[:, 128 * n : 128 * n + 128] for n in (r, 2 + r)])
            part[r, g] = sent[:, :384]
            msg[r, g // 2, g % 2] = beside([sent[:, 128 : 128 + B], sent[:, 256 : 256 + B]]).astype(BF16)
        for c in some:
            for r in range(2):
                msg[r, c, 2] = beside([leave[r, 2 * c + i][:, 384 : 384 + B] for i in range(2)]).astype(BF16)
            depart(c, 0)

    def last_step(c):
        for r in range(2):

            @pl.when(there[r])
            def _():
                ps_copy(r, c, True).wait_recv()

        leave = {}
        none = beside([tile0] * 3)
        for r, i in units:
            even, odd = outside(r, 2 * c + i)
            right = below([none, even, none, odd] if r == 0 else [even, none, odd, none])
            leave[r, i] = jnp.dot(facing[r, 2 * c + i], right, preferred_element_type=F32)
        for r, i in units:
            sent = part[r, 2 * c + i] + leave[r, i]
            msg[r, c, 3 + 2 * i] = sent[:, :128].astype(BF16)
            msg[r, c, 4 + 2 * i] = beside([sent[:, 128 + B : 256], sent[:, 256 + B :]]).astype(BF16)
        depart(c, 1)

    def own_step(some):
        value, made = {}, {}
        every = [(r, g) for g in some for r in range(2)]
        for r, g in every:
            value[r, g] = jnp.dot(staying(r, g), operator(r, g), preferred_element_type=F32).astype(BF16)
        for r, g in every:
            made[r, g] = jnp.dot(value[r, g], columns(r, g, True), preferred_element_type=F32)
        for g in some:
            spread_out(g, made[0, g], made[1, g])

    def depart(c, late):
        @pl.when(jnp.logical_and(slow == 1, there[1]))
        def _():
            ms_copy(1, c, late).start()

        @pl.when(there[0])
        def _():
            ms_copy(0, c, late).start()

        @pl.when(jnp.logical_and(slow == 0, there[1]))
        def _():
            ms_copy(1, c, late).start()

    ends, middle = [0, chunks - 1], list(range(1, chunks - 1))
    if middle:
        first_step(middle)

    for d in (2, 3):

        @pl.when(there[d])
        def _():
            sp_copy(d, True).wait_recv()

    for d, at, column in ((2, 0, cols - 1), (3, cols + 1, 0)):
        for r in range(2):
            spill = jnp.broadcast_to(sp_h[d, r : r + 1, column : column + 1].astype(F32), (16, 128)).astype(BF16)
            m0t[1 + r, at] = (1.0 - spill) * reach[r]
            m1t[1 + r, at] = spill

    for d in (2, 3):

        @pl.when(there[d])
        def _():
            pg_copy(d, True).wait_recv()

    first_step(ends)
    for d in (0, 1):

        @pl.when(there[d])
        def _():
            sp_copy(d, True).wait_recv()

    masks_of_row(sp_h[0, 1:2].astype(F32), 0)
    masks_of_row(sp_h[1, 0:1].astype(F32), 3)


    def spread_out(g, before, after):
        def tiles(rows):
            b, a = (
                [x[B * rows : B * rows + B, 128 * n : 128 * n + 128] for n in range(4)] for x in (before, after)
            )
            return b[0] + a[3], a[0] + b[3], b[1] + a[1], b[2], a[2]

        um, up, ce, d0, d1 = (swap_halves(x) for x in tiles(0))
        acc[g, 0] = jnp.where(low, d0, um)
        acc[g, 1] = jnp.where(low, um, 0.0)
        acc[g, 2] = jnp.where(low, 0.0, ce)
        acc[g, 3] = jnp.where(low, ce, d0 + d1)
        acc[g, 4] = jnp.where(low, d1, up)
        acc[g, 5] = jnp.where(low, up, 0.0)
        um, up, ce, d0, d1 = tiles(1)
        gr[g, 0] = jnp.where(low, um, d0).astype(BF16)
        gr[g, 1] = jnp.where(low, up, d1).astype(BF16)
        gr[g, 2] = ce.astype(BF16)
        gr[g, 3] = jnp.where(low, d0 + d1, 0.0).astype(BF16)
        um, up, ce, d0, d1 = tiles(2)
        gl[g + 1, 0] = um.astype(BF16)
        gl[g + 1, 1] = up.astype(BF16)
        gl[g + 1, 2] = ce.astype(BF16)
        gl[g + 1, 3] = (d0 + d1).astype(BF16)

    def nth(t):
        return jnp.where(t == 0, 0, jnp.where(t == 1, chunks - 1, t - 1))

    def late_step(t, carry):
        last_step(nth(t))
        return carry

    lax.fori_loop(0, 2, late_step, 0)
    own_step([0, aggs - 1])
    for d in (2, 3):

        @pl.when(there[d])
        def _():
            mg_copies[d].start()

    lax.fori_loop(2, chunks, late_step, 0)
    inner_aggs = list(range(1, aggs - 1))
    for first in range(0, aggs - 2, 3):
        own_step(inner_aggs[first : first + 3])
    for d in (2, 3):

        @pl.when(there[d])
        def _():
            mg_landing[d].wait_recv()

    def finish(c):
        for d in range(2):

            @pl.when(there[d])
            def _():
                for late in range(2):
                    ms_copy(d, c, late, True).wait_recv()

        for i in range(2):
            g = 2 * c + i
            be, bz, fe, fz = (rmsg[d, c, n].astype(F32) for d in range(2) for n in (i, 4 + 2 * i))
            b0, f0 = (rmsg[d, c, 3 + 2 * i].astype(F32) for d in range(2))
            b3, f3 = (rmsg[d, c, 2].astype(F32) for d in range(2))
            if i == 1:
                b3, f3 = swap_halves(b3), swap_halves(f3)
            b1, f1 = jnp.where(low, be, swap_halves(bz)), jnp.where(low, fe, swap_halves(fz))
            b2, f2 = jnp.where(low, swap_halves(be), bz), jnp.where(low, swap_halves(fe), fz)
            l0, l1, l2, l3 = (gl[g, n].astype(F32) for n in range(4))
            r0, r1, r2, r3 = (gr[g + 1, n].astype(F32) for n in range(4))
            tiles = (
                (1, jnp.where(low, b3, 0.0)),
                (3, acc[g, 0] + b1 + l0 + jnp.where(low, 0.0, r0)),
                (4, acc[g, 1] + jnp.where(low, b2 + r0, 0.0)),
                (5, acc[g, 2] + l2 + jnp.where(low, 0.0, b2 + f2)),
                (6, acc[g, 3] + b0 + f0 + l3 + r2),
                (7, r3),
                (8, acc[g, 4] + f1 + l1 + jnp.where(low, 0.0, r1)),
                (9, acc[g, 5] + jnp.where(low, f2 + r1, 0.0)),
                (11, jnp.where(low, f3, 0.0)),
            )
            for t, value in tiles:
                out[0, g, :, 128 * t : 128 * t + 128] = value.astype(BF16)

    for c in order:
        finish(c)

    for d in range(4):

        @pl.when(there[d])
        def _():
            sp_copy(d).wait_send()
            if d < 2:
                for c in range(chunks):
                    ps_copy(d, c).wait_send()
                    for late in range(2):
                        ms_copy(d, c, late).wait_send()
            else:
                pg_copy(d).wait_send()
                mg_copies[d].wait_send()


def local(a_vals, p_vals, spill_axis):
    n_sub = lax.axis_size("sub")
    n_gy = lax.axis_size("gy")
    cols = a_vals.shape[1]
    aggs = cols // 2
    chunks = aggs // 2
    dma = pltpu.SemaphoreType.DMA
    return pl.pallas_call(
        functools.partial(kernel, n_sub, n_gy, cols),
        out_shape=jax.ShapeDtypeStruct((1, aggs, B, SLOTS * B), BF16),
        in_specs=[pl.BlockSpec(memory_space=pl.ANY)] * 3,
        out_specs=pl.BlockSpec(memory_space=pltpu.VMEM),
        scratch_shapes=[
            pltpu.VMEM((2, cols, B, 5 * B), BF16),
            pltpu.VMEM((4, cols + 2, B, 128), BF16),
            pltpu.VMEM((2, cols), jnp.int32),
            pltpu.VMEM((4, 2, cols), jnp.int32),
            pltpu.VMEM((4, cols + 2, 16, 128), BF16),
            pltpu.VMEM((4, cols + 2, 16, 128), BF16),
            pltpu.VMEM((2, cols, B, 128), BF16),
            pltpu.VMEM((2, aggs, 128, 128), BF16),
            pltpu.VMEM((2, aggs, B, 384), F32),
            pltpu.VMEM((2, aggs, B, 256), BF16),
            pltpu.VMEM((2, chunks, 7, B, 128), BF16),
            pltpu.VMEM((2, chunks, 7, B, 128), BF16),
            pltpu.VMEM((aggs, 6, B, 128), F32),
            pltpu.VMEM((aggs + 1, 4, B, 128), BF16),
            pltpu.VMEM((aggs + 1, 4, B, 128), BF16),
            dma((3,)),
            dma((4,)),
            dma((4,)),
            dma((2, chunks)),
            dma((2, chunks)),
            dma((2,)),
            dma((2,)),
            dma((2, chunks, 2)),
            dma((2, chunks, 2)),
            dma((2,)),
            dma((2,)),
        ],
        compiler_params=pltpu.CompilerParams(
            collective_id=0, has_side_effects=True, vmem_limit_bytes=40 * 1024 * 1024
        ),
        cost_estimate=pl.CostEstimate(flops=1_300_000_000, bytes_accessed=4_000_000, transcendentals=0),
    )(*(pltpu.with_memory_space_constraint(x, pltpu.HBM) for x in (a_vals, p_vals, spill_axis)))


def solution(mesh):
    return jax.shard_map(
        local,
        mesh=mesh,
        in_specs=(P("sub", "gy", None, None), P("sub", "gy", None, None), P("sub", "gy")),
        out_specs=P("sub", "gy", None, None),
        check_vma=False,
    )
```
